32 devices in a mesh: tile: 8 (over z, x), filt: 4 (over y, core).
Axes of the slice: x: 2, y: 2, z: 4, core: 2. Of those that a mesh axis runs over, the one named last changes fastest.
Arguments:
- panels: bfloat16 [64, 12, 512], P('tile', None, 'filt'), may hold values from -12 to 12
- panel_tile: int32 [64, 1], P('tile'), may hold values from 0 to 7; in each aligned block of 8 rows (0 to 7, 8 to 15, ...) at most 2 rows name the same one
- panel_date: int32 [64], P('tile'), may hold values from 0 to 1
- stem_weight: bfloat16 [12, 128], replicated, may hold values from -1.75 to 1.75
- spatial_weight: bfloat16 [3, 3, 128, 128], P(None, None, None, 'filt'), may hold values from -0.1875 to 0.1875
- temporal_weight: bfloat16 [3, 128, 128], P(None, None, 'filt'), may hold values from -0.3125 to 0.3125
- cotangent: bfloat16 [2, 128, 32, 128], P(None, 'filt', 'tile'), may hold values from -6 to 6
Outputs:
- features_out: bfloat16 [2, 128, 32, 128], P(None, 'filt', 'tile')
- grad_stem: float32 [12, 128], replicated
- grad_spatial: float32 [3, 3, 128, 128], P(None, None, None, 'filt')
- grad_temporal: float32 [3, 128, 128], P(None, None, 'filt')
- band_grad: float32 [2, 12, 4096], P(None, None, ('tile', 'filt'))
The draws below stay inside these ranges and needn't reach their ends.
Inputs may be any that keep to these rules, and one draw needn't show every extreme that they name: `panel_tile`: among the panels of one reader (aligned blocks of 8 rows) no tile is named more than 2 times, a bound that some block reaches.
All inputs are finite; a program needn't handle non-finite values.
Results may differ from the reference program's by a relative error of at most 0.015.
Values may be sent and summed in bfloat16 or wider, within the bound.
A program may use at most 64 MiB of HBM per device.

```python
import math
import jax
import jax.numpy as jnp
import numpy as np
from jax import lax

C = 128
BANDS = 12
DATES = 2
ROWS_DEV = 4
COLS = 128
CAP = 2
SLOTS = 8
PANELS = 64
NROWS = 32
N_TILE = 8
N_FILT = 4


def place_ends(array, own_key, low, top_value):
    longest = array.shape.index(max(array.shape))
    spots = []
    for shift in (0, 1):
        where = [jax.random.randint(jax.random.fold_in(own_key, axis), (), 0, length) for axis, length in enumerate(array.shape)]
        where[longest] = (where[longest] + shift) % array.shape[longest]
        spots.append(tuple(where))
    return array.at[spots[0]].set(low).at[spots[1]].set(top_value)


def levels(rng, shape, cuts, low, top_value):
    factor_of, own = 1.0, jax.random.fold_in(rng, 6)
    for position, shards_of in cuts:
        heights = jnp.exp(jax.random.uniform(jax.random.fold_in(own, position), (shards_of,), jnp.float32, low / len(cuts), top_value / len(cuts)))
        factor_of = factor_of * jnp.repeat(heights, shape[position] // shards_of).reshape([-1 if axis == position else 1 for axis in range(len(shape))])
    return factor_of


def assign_block(stream_key, own, number, rows, amount, top, most, lean):
    order = jax.random.permutation(stream_key, amount)
    packed, usual = portions_of(amount, rows * top, most, lean, True), portions_of(amount, rows * top, most, lean, False)
    places = jnp.arange(amount)

    def named(tallies, offset_by):
        used = int((tallies > 0).sum())
        fixed = max(1, used // 4)
        shifted = fixed + (places - fixed + offset_by * (used - fixed)) % max(1, amount - fixed)
        return jnp.zeros((amount,), jnp.int32).at[order[jnp.where(places < fixed, places, shifted)]].set(jnp.asarray(tallies, jnp.int32))

    tallies = jnp.where(number % 4 == 0, named(packed, number // 4), named(usual, number - number // 4 - 1))
    mixed = jax.random.permutation(jax.random.fold_in(own, 3), amount)
    source_of, taker = mixed[0:amount // 2 * 2:2], mixed[1:amount // 2 * 2:2]
    room = jnp.minimum(tallies[source_of] - 1, most - tallies[taker]) // 2
    room = jnp.where((source_of == order[0]) | (taker == order[0]) | (tallies[taker] == 0), 0, jnp.maximum(room, 0))
    shifted = jax.random.randint(jax.random.fold_in(own, 4), (amount // 2,), 0, 1 << 20) % (room + 1)
    tallies = tallies.at[source_of].add(-shifted).at[taker].add(shifted)
    members = jnp.searchsorted(jnp.cumsum(tallies), jnp.arange(rows * top), side="right").astype(jnp.int32)
    grid = members.reshape(top, rows).T
    grid = grid[jax.random.permutation(jax.random.fold_in(own, 1), rows)]
    offset_by = jax.random.randint(jax.random.fold_in(own, 2), (rows, 1), 0, top)
    return jnp.take_along_axis(grid, (jnp.arange(top)[None, :] + offset_by) % top, axis=1)


def portions_of(count, total, limit, skew, full):
    portions = [(1 << 20) // math.isqrt(grade ** skew) + 1 for grade in range(1, count + 1)]
    largest = limit if full else min(limit, max(-(-total // count), total * portions[0] // sum(portions)))
    least = 1 if total - largest >= count - 1 else 0
    holding, rest = [largest] + [least] * (count - 1), total - largest - least * (count - 1)
    while rest > 0:
        candidates = [i for i in range(1, count) if holding[i] < largest] or [i for i in range(1, count) if holding[i] < limit]
        mass, left = sum([portions[i] for i in candidates]), rest
        for i in candidates:
            extra = min(limit - holding[i], max(1, left * portions[i] // mass), rest)
            holding[i] = holding[i] + extra
            rest = rest - extra
    return np.array(holding)


def gaussian(stream_key, dims, scale, reach, split=(), kind=jnp.bfloat16):
    result = jax.random.normal(stream_key, dims, jnp.float32) * scale
    if len(split) > 0:
        result = levels(stream_key, dims, split, -0.22, 0.18) * result
    return jnp.clip(result, min=-reach, max=reach).astype(kind)


def setup_inputs(seed: int = 0) -> dict:
    keys = jax.random.split(jax.random.key(seed), 8)
    panels = gaussian(keys[0], (PANELS, BANDS, ROWS_DEV * COLS), 2.0, 12.0, ((0, 8), (2, 4)))
    panel_tile_keys = jax.random.split(jax.random.fold_in(keys[1], 1), PANELS // SLOTS)
    panel_tile_turns = jax.random.permutation(jax.random.fold_in(keys[1], 3), PANELS // SLOTS)
    panel_tile = jax.vmap(lambda own, number: assign_block(jax.random.fold_in(keys[1], 2), own, number, SLOTS, N_TILE, 1, CAP, 2))(panel_tile_keys, panel_tile_turns).reshape((PANELS, 1))
    panel_date = place_ends(jax.random.randint(keys[2], (PANELS,), 0, DATES), jax.random.fold_in(keys[2], 1), 0, DATES - 1).astype(jnp.int32)
    stem_weight = gaussian(keys[3], (BANDS, C), BANDS ** -0.5, 1.75)
    spatial_weight = gaussian(keys[4], (3, 3, C, C), (9 * C) ** -0.5, 0.1875, ((3, 4),))
    temporal_weight = gaussian(keys[5], (3, C, C), (3 * C) ** -0.5, 0.3125, ((2, 4),))
    cotangent = gaussian(keys[6], (DATES, C, NROWS, COLS), 1.0, 6.0, ((1, 4), (2, 8)))
    return {"panels": panels, "panel_tile": panel_tile, "panel_date": panel_date, "stem_weight": stem_weight, "spatial_weight": spatial_weight, "temporal_weight": temporal_weight, "cotangent": cotangent}


def spatial_conv(inputs, kernel):
    return lax.conv_general_dilated(inputs, kernel, (1, 1), ((1, 1), (1, 1)), dimension_numbers=('NCHW', 'HWIO', 'NCHW'), precision=lax.Precision.HIGHEST)

def silu_slope(pre_act):
    sigma = jax.nn.sigmoid(pre_act)
    return sigma * (1.0 + pre_act * (1.0 - sigma))

def rounded(values):
    return lax.optimization_barrier(values.astype(jnp.bfloat16)).astype(jnp.float32)

def reference(panels, panel_tile, panel_date, stem_weight, spatial_weight, temporal_weight, cotangent):
    highest = lax.Precision.HIGHEST
    seg_ids = (panel_tile[:, 0] * DATES + panel_date).astype(jnp.int32)
    date_sums = jax.ops.segment_sum(panels.astype(jnp.float32), seg_ids, num_segments=N_TILE * DATES)
    date_counts = jax.ops.segment_sum(jnp.ones(seg_ids.shape, jnp.float32), seg_ids, num_segments=N_TILE * DATES)
    tile_images = (date_sums / jnp.maximum(date_counts, 1.0)[:, None, None]).astype(jnp.bfloat16)
    raw_bands = tile_images.reshape(N_TILE, DATES, BANDS, ROWS_DEV, COLS).transpose(1, 2, 0, 3, 4).reshape(DATES, BANDS, NROWS, COLS)
    raw_float = raw_bands.astype(jnp.float32)
    stem_float = stem_weight.astype(jnp.float32)
    features = jnp.einsum('bc,tbrw->tcrw', stem_float, raw_float, precision=highest).astype(jnp.bfloat16)
    feat_float = features.astype(jnp.float32)
    spatial_float = spatial_weight.astype(jnp.float32)
    pre_act = spatial_conv(feat_float, spatial_float)
    activated = jax.nn.silu(pre_act).astype(jnp.bfloat16)
    zero_date = jnp.zeros((1, C, NROWS, COLS), jnp.float32)
    act_pad = jnp.concatenate([zero_date, activated.astype(jnp.float32), zero_date], axis=0)
    temporal_float = temporal_weight.astype(jnp.float32)
    temporal_out = jnp.zeros((DATES, C, NROWS, COLS), jnp.float32)
    for lag in range(3):
        temporal_out = temporal_out + jnp.einsum('tirw,io->torw', act_pad[lag:lag + DATES], temporal_float[lag], precision=highest)
    features_out = (feat_float + temporal_out).astype(jnp.bfloat16)
    grad_float = cotangent.astype(jnp.float32)
    grad_scale = 1.0 / math.sqrt(DATES * NROWS * COLS)
    grad_temporal = jnp.stack([jnp.einsum('tirw,torw->io', act_pad[lag:lag + DATES], grad_float, precision=highest) for lag in range(3)]) * grad_scale
    grad_pad = jnp.concatenate([zero_date, grad_float, zero_date], axis=0)
    group_width = C // N_FILT
    act_grad = jnp.zeros((DATES, C, NROWS, COLS), jnp.float32)
    for group in range(N_FILT):
        low = group * group_width
        part_sum = jnp.zeros((DATES, C, NROWS, COLS), jnp.float32)
        for lag in range(3):
            part_sum = part_sum + jnp.einsum('torw,io->tirw', grad_pad[2 - lag:2 - lag + DATES, low:low + group_width], temporal_float[lag][:, low:low + group_width], precision=highest)
        act_grad = act_grad + rounded(part_sum)
    pre_grad = (act_grad * silu_slope(pre_act)).astype(jnp.bfloat16)
    pre_float = pre_grad.astype(jnp.float32)
    unused_out, kernel_vjp = jax.vjp(lambda kernel: spatial_conv(feat_float, kernel), spatial_float)
    grad_spatial = kernel_vjp(pre_float)[0] * grad_scale
    feat_grad = jnp.zeros((DATES, C, NROWS, COLS), jnp.float32)
    for group in range(N_FILT):
        low = group * group_width
        group_kernel = spatial_float[:, :, :, low:low + group_width]
        unused_out, input_vjp = jax.vjp(lambda inputs: spatial_conv(inputs, group_kernel), feat_float)
        part_sum = input_vjp(pre_float[:, low:low + group_width])[0]
        part_sum = part_sum.at[:, low:low + group_width].add(grad_float[:, low:low + group_width])
        feat_grad = feat_grad + rounded(part_sum)
    grad_stem = jnp.einsum('tbrw,tcrw->bc', raw_float, feat_grad, precision=highest) * grad_scale
    band_grad = jnp.einsum('bc,tcrw->tbrw', stem_float, feat_grad, precision=highest).reshape(DATES, BANDS, NROWS * COLS)
    return (features_out, grad_stem, grad_spatial, grad_temporal, band_grad)
```

```python
import functools
import math

import jax
import jax.numpy as jnp
from jax import lax
from jax.experimental import pallas as pl
from jax.experimental.pallas import tpu as pltpu
from jax.sharding import PartitionSpec as P

MESH = pl.DeviceIdType.MESH
F32 = jnp.float32
BF16 = jnp.bfloat16


def loop(count, body):
    if count <= 8:
        for i in range(count):
            body(i)
    else:
        lax.fori_loop(0, count, lambda i, c: (body(i), c)[1], 0)


def total(count, term):
    if count <= 8:
        out = term(0)
        for i in range(1, count):
            out = out + term(i)
        return out
    return lax.fori_loop(1, count, lambda i, c: c + term(i), term(0))


def dot(a, b):
    return jnp.dot(a, b, preferred_element_type=F32)


def dot_t(a, b):
    return lax.dot_general(a, b, (((1,), (1,)), ((), ())), preferred_element_type=F32)


def shifted(block, offset):
    cols = block.shape[1]
    lane = lax.broadcasted_iota(jnp.int32, block.shape, 1)
    if offset == 1:
        return jnp.where(lane == cols - 1, 0.0, pltpu.roll(block, cols - 1, 1))
    return jnp.where(lane == 0, 0.0, pltpu.roll(block, 1, 1))


def kernel(
    n, nf, bp, scale,
    tile_ref, date_ref, panels_ref, stem_ref, wt_ref, cot_ref,
    fo_ref, gstem_ref, gsp_ref, gtm_ref, bg_ref,
    pp, pan_out, pan_in, raw, wall, wback, stem16, stem_t, cot, feat, act, pre_g, pg3,
    rs_out, rs_in, ag, sa_out, sa, sb_out, sb,
    pan_s, pan_r, raw_s, raw_r, w_s, w_r, c_s, c_r, lo_s, lo_r, hi_s, hi_r,
    rs_s, rs_r, ag_s, ag_r, sa_s, sa_r, sb_s, sb_r,
):
    j = lax.axis_index("tile")
    f = lax.axis_index("filt")
    n_slots = panels_ref.shape[0]
    bands = panels_ref.shape[1]
    own = wt_ref.shape[0]
    chan = own * nf
    cols = 128

    def tpeer(d):
        return lax.rem(j + d, n)

    def fpeer(d):
        return lax.rem(f + d, nf)

    def remote(src, dst, s, r, to):
        return pltpu.make_async_remote_copy(
            src_ref=src, dst_ref=dst, send_sem=s, recv_sem=r, device_id=to, device_id_type=MESH
        )

    barrier = pltpu.get_barrier_semaphore()

    def hello(t, g):
        pl.semaphore_signal(barrier, inc=1, device_id=(t, g), device_id_type=MESH)

    loop(n - 1, lambda d: hello(tpeer(d + 1), f))
    for d in range(1, nf):
        hello(j, fpeer(d))

    @pl.when(j > 0)
    def _():
        for d in range(1, nf):
            hello(j - 1, fpeer(d))

    @pl.when(j < n - 1)
    def _():
        for d in range(1, nf):
            hello(j + 1, fpeer(d))

    pad_rows = lax.broadcasted_iota(jnp.int32, (n_slots, 16, cols), 1)
    pp[...] = jnp.where(pad_rows == bands, 1.0, 0.0)
    pp[:, 0:bands, :] = panels_ref[...].astype(F32)

    def fill(k):
        def term(s):
            block = pp[s]
            here = tile_ref[s, 0] == k
            first = jnp.where(here & (date_ref[s] == 0), 1.0, 0.0)
            second = jnp.where(here & (date_ref[s] == 1), 1.0, 0.0)
            return jnp.concatenate([block * first, block * second], axis=0)

        pan_out[k] = total(n_slots, term).astype(BF16)

    loop(n, fill)

    @pl.when(j == 0)
    def _():
        raw[0:2] = jnp.zeros((2, 32, cols), BF16)
        cot[0] = jnp.zeros((2, chan, cols), BF16)

    @pl.when(j == n - 1)
    def _():
        raw[6:8] = jnp.zeros((2, 32, cols), BF16)
        cot[5] = jnp.zeros((2, chan, cols), BF16)

    sides = jnp.where(j > 0, 1, 0) + jnp.where(j < n - 1, 1, 0)
    pl.semaphore_wait(barrier, n - 1 + (nf - 1) * (1 + sides))

    def pan_copy(d):
        k = tpeer(d)
        return remote(pan_out.at[k], pan_in.at[j], pan_s.at[d], pan_r.at[j], (k, f))

    def pan_wait(d):
        k = tpeer(d)
        remote(pan_out.at[k], pan_in.at[k], pan_s.at[d], pan_r.at[k], (k, f)).wait_recv()

    loop(n - 1, lambda d: pan_copy(d + 1).start())

    mine = pl.ds(pl.multiple_of(f * own, own), own)

    def w_copy(d):
        return remote(wt_ref, wall.at[mine], w_s.at[d], w_r.at[f], (j, fpeer(d)))

    def c_copy(d):
        return remote(cot_ref, cot.at[pl.ds(1, 4), :, mine, :], c_s.at[d], c_r.at[f], (j, fpeer(d)))

    def lo_copy(d):
        return remote(cot_ref.at[3], cot.at[0, :, mine, :], lo_s.at[d], lo_r.at[f], (j + 1, fpeer(d)))

    def hi_copy(d):
        return remote(cot_ref.at[0], cot.at[5, :, mine, :], hi_s.at[d], hi_r.at[f], (j - 1, fpeer(d)))

    for d in range(1, nf):
        w_copy(d).start()
    for d in range(1, nf):
        c_copy(d).start()

    @pl.when(j < n - 1)
    def _():
        for d in range(nf):
            lo_copy(d).start()

    @pl.when(j > 0)
    def _():
        for d in range(nf):
            hi_copy(d).start()

    wall[mine, :] = wt_ref[...]
    cot[1:5, :, mine, :] = cot_ref[...]
    stem_t[...] = jnp.zeros((cols, chan), F32)
    stem_t[0:bands, :] = stem_ref[...].astype(F32)
    stem16[...] = stem_t[0:16, :].astype(BF16)
    stem_lhs = stem_t[...].T[:, 0:16].astype(BF16)

    pan_in[j] = pan_out[j]
    loop(n - 1, lambda d: pan_wait(d + 1))
    sums = total(n, lambda k: pan_in[k].astype(F32))
    row = jnp.concatenate(
        [
            sums[t * 16 : t * 16 + 16] / jnp.maximum(sums[t * 16 + bands : t * 16 + bands + 1], 1.0)
            for t in range(2)
        ],
        axis=0,
    ).astype(BF16)
    raw[2 + f] = row

    def raw_copy(d):
        return remote(raw.at[2 + f], raw.at[2 + f], raw_s.at[d], raw_r.at[2 + f], (j, fpeer(d)))

    def raw_down(d):
        return remote(raw.at[2 + f], raw.at[f - 2], raw_s.at[4 + d], raw_r.at[f - 2], (j + 1, fpeer(d)))

    def raw_up(d):
        return remote(raw.at[2 + f], raw.at[6 + f], raw_s.at[4 + d], raw_r.at[6 + f], (j - 1, fpeer(d)))

    for d in range(1, nf):
        raw_copy(d).start()
    goes_down = (f >= 2) & (j < n - 1)
    goes_up = (f < 2) & (j > 0)

    @pl.when(goes_down)
    def _():
        for d in range(nf):
            raw_down(d).start()

    @pl.when(goes_up)
    def _():
        for d in range(nf):
            raw_up(d).start()

    for d in range(1, nf):
        g = fpeer(d)
        theirs = pl.ds(pl.multiple_of(g * own, own), own)
        remote(wt_ref, wall.at[theirs], w_s.at[d], w_r.at[g], (j, g)).wait_recv()
    for q in range(12):
        block = wall[:, q * chan : (q + 1) * chan].astype(F32).T.astype(BF16)
        at = q if q < 9 else 9 + (11 - q)
        wback[:, at * chan : (at + 1) * chan] = block

    def raw_wait(slot):
        remote(raw.at[slot], raw.at[slot], raw_s.at[0], raw_r.at[slot], (j, fpeer(1))).wait_recv()

    for d in range(1, nf):
        raw_wait(2 + fpeer(d))

    @pl.when(j > 0)
    def _():
        raw_wait(0)
        raw_wait(1)

    @pl.when(j < n - 1)
    def _():
        raw_wait(6)
        raw_wait(7)

    for t in range(2):
        for r in range(8):
            block = dot(stem_lhs, raw[r, t * 16 : t * 16 + 16, :]).astype(BF16)
            at = (t * 8 + r) * cols
            wide = block.astype(F32)
            feat[0:chan, at : at + cols] = shifted(wide, -1).astype(BF16)
            feat[chan : 2 * chan, at : at + cols] = block
            feat[2 * chan : 3 * chan, at : at + cols] = shifted(wide, 1).astype(BF16)

    for d in range(1, nf):
        g = fpeer(d)
        theirs = pl.ds(pl.multiple_of(g * own, own), own)
        remote(cot_ref, cot.at[pl.ds(1, 4), :, theirs, :], c_s.at[d], c_r.at[g], (j, g)).wait_recv()

    @pl.when(j > 0)
    def _():
        for g in range(nf):
            remote(cot_ref.at[3], cot.at[0, :, g * own : (g + 1) * own, :], lo_s.at[g], lo_r.at[g], (j - 1, g)).wait_recv()

    @pl.when(j < n - 1)
    def _():
        for g in range(nf):
            remote(cot_ref.at[0], cot.at[5, :, g * own : (g + 1) * own, :], hi_s.at[g], hi_r.at[g], (j + 1, g)).wait_recv()

    cot_rows = jnp.concatenate([cot[r].reshape(2 * chan, cols) for r in range(6)], axis=1)
    lane = lax.broadcasted_iota(jnp.int32, (chan, 6 * cols), 1)
    inside = ((lane >= cols) | (j > 0)) & ((lane < 5 * cols) | (j < n - 1))
    for t in range(2):
        pre = dot(wall[:, 0 : 3 * chan], feat[:, t * 1024 : t * 1024 + 768])
        for dy in (1, 2):
            at = t * 1024 + dy * cols
            pre = pre + dot(wall[:, dy * 3 * chan : (dy + 1) * 3 * chan], feat[:, at : at + 768])
        sigma = jax.nn.sigmoid(pre)
        act[t * chan : (t + 1) * chan, :] = (pre * sigma)[:, cols : 5 * cols].astype(BF16)
        act_grad = dot(wback[:, (10 - t) * chan : (12 - t) * chan], cot_rows)
        slope = sigma * (1.0 + pre * (1.0 - sigma))
        pre_g[:, t * 768 : (t + 1) * 768] = jnp.where(inside, act_grad * slope, 0.0).astype(BF16)

    def put(q, grad):
        for h in range(2):
            b = q * 2 + h
            rs_out[b // bp, (b % bp) * 16 : (b % bp) * 16 + 16, :] = grad[h * 16 : h * 16 + 16].astype(BF16)

    cot_own = [
        jnp.concatenate([cot_ref[r, t] for r in range(4)], axis=1) for t in range(2)
    ]
    act0, act1 = act[0:chan, :], act[chan : 2 * chan, :]
    put(9, dot_t(cot_own[1], act0) * scale)
    put(10, (dot_t(cot_own[0], act0) + dot_t(cot_own[1], act1)) * scale)
    put(11, dot_t(cot_own[0], act1) * scale)
    pg_own = [pre_g[mine, t * 768 + cols : t * 768 + 5 * cols] for t in range(2)]
    for dy in range(3):
        at = (dy + 1) * cols
        grad = dot_t(pg_own[0], feat[:, at : at + 512])
        grad = grad + dot_t(pg_own[1], feat[:, 1024 + at : 1024 + at + 512])
        grad = grad * scale
        for dx in range(3):
            put(dy * 3 + dx, grad[:, dx * chan : (dx + 1) * chan])
    if n * bp > 24:
        used = -(-24 // bp)
        loop(n - used, lambda k: rs_out.__setitem__(used + k, jnp.zeros((bp * 16, cols), BF16)))

    def rs_copy(d):
        k = tpeer(d)
        return remote(rs_out.at[k], rs_in.at[j], rs_s.at[d], rs_r.at[j], (k, f))

    loop(n - 1, lambda d: rs_copy(d + 1).start())
    rs_in[j] = rs_out[j]

    for t in range(2):
        for r in range(3):
            at = pl.ds(pl.multiple_of(t * 768 + (f + r) * cols, cols), cols)
            block = pre_g[:, at]
            wide = block.astype(F32)
            to = (r * 2 + t) * cols
            pg3[0:chan, to : to + cols] = shifted(wide, 1).astype(BF16)
            pg3[chan : 2 * chan, to : to + cols] = block
            pg3[2 * chan : 3 * chan, to : to + cols] = shifted(wide, -1).astype(BF16)
    fgrad = jnp.concatenate([cot[1 + f, t].astype(F32) for t in range(2)], axis=1)
    for dy in range(3):
        at = (2 - dy) * 2 * cols
        fgrad = fgrad + dot(wback[:, dy * 3 * chan : (dy + 1) * 3 * chan], pg3[:, at : at + 2 * cols])
    upper = fgrad.astype(BF16)
    lower = (fgrad - upper.astype(F32)).astype(BF16)
    own_raw = raw[2 + f]
    raw_row = jnp.concatenate([own_raw[0:16], own_raw[16:32]], axis=1)
    sa_out[...] = (dot_t(raw_row, upper) + dot_t(raw_row, lower)) * scale

    def sa_copy(d):
        return remote(sa_out, sa.at[f], sa_s.at[d], sa_r.at[f], (j, fpeer(d)))

    for d in range(1, nf):
        sa_copy(d).start()
    sa[f] = sa_out[...]
    bgrad = dot(stem16[...], upper) + dot(stem16[...], lower)
    for t in range(2):
        bg_ref[t] = bgrad[0:bands, t * cols : (t + 1) * cols]

    wt_time = wt_ref[:, 9 * chan : 12 * chan]
    feat_own = pl.ds(pl.multiple_of(chan + f * own, own), own)
    for t in range(2):
        out = dot(wt_time[:, (1 - t) * chan : (3 - t) * chan], act[...])
        out = out + feat[feat_own, t * 1024 + 256 : t * 1024 + 768].astype(F32)
        for r in range(4):
            fo_ref[t, r] = out[:, r * cols : (r + 1) * cols].astype(BF16)

    for d in range(1, nf):
        g = fpeer(d)
        remote(sa_out, sa.at[g], sa_s.at[d], sa_r.at[g], (j, g)).wait_recv()
    sb_out[...] = (sa[0] + sa[1]) + (sa[2] + sa[3])

    def sb_copy(d):
        k = tpeer(d)
        return remote(sb_out, sb.at[j], sb_s.at[d], sb_r.at[j], (k, f))

    loop(n - 1, lambda d: sb_copy(d + 1).start())
    sb[j] = sb_out[...]

    def rs_wait(d):
        k = tpeer(d)
        remote(rs_out.at[k], rs_in.at[k], rs_s.at[d], rs_r.at[k], (k, f)).wait_recv()

    loop(n - 1, lambda d: rs_wait(d + 1))
    ag[j] = total(n, lambda k: rs_in[k].astype(F32)).astype(BF16)

    def ag_copy(d):
        k = tpeer(d)
        return remote(ag.at[j], ag.at[j], ag_s.at[d], ag_r.at[j], (k, f))

    loop(n - 1, lambda d: ag_copy(d + 1).start())

    loop(n - 1, lambda d: pan_copy(d + 1).wait_send())
    for d in range(1, nf):
        w_copy(d).wait_send()
        c_copy(d).wait_send()
        raw_copy(d).wait_send()
        sa_copy(d).wait_send()

    @pl.when(j < n - 1)
    def _():
        for d in range(nf):
            lo_copy(d).wait_send()

    @pl.when(j > 0)
    def _():
        for d in range(nf):
            hi_copy(d).wait_send()

    @pl.when(goes_down)
    def _():
        for d in range(nf):
            raw_down(d).wait_send()

    @pl.when(goes_up)
    def _():
        for d in range(nf):
            raw_up(d).wait_send()

    loop(n - 1, lambda d: rs_copy(d + 1).wait_send())

    def sb_wait(d):
        k = tpeer(d)
        remote(sb_out, sb.at[k], sb_s.at[d], sb_r.at[k], (k, f)).wait_recv()

    loop(n - 1, lambda d: sb_wait(d + 1))
    gstem_ref[...] = total(n, lambda k: sb[k])[0:bands]

    def ag_wait(d):
        k = tpeer(d)
        remote(ag.at[k], ag.at[k], ag_s.at[d], ag_r.at[k], (k, f)).wait_recv()

    loop(n - 1, lambda d: ag_wait(d + 1))
    for q in range(12):
        halves = []
        for h in range(2):
            b = q * 2 + h
            halves.append(ag[b // bp, (b % bp) * 16 : (b % bp) * 16 + 16, :].astype(F32))
        block = jnp.concatenate(halves, axis=0).T
        if q < 9:
            gsp_ref[q] = block
        else:
            gtm_ref[q - 9] = block
    loop(n - 1, lambda d: ag_copy(d + 1).wait_send())
    loop(n - 1, lambda d: sb_copy(d + 1).wait_send())


def per_device(
    panels, panel_tile, panel_date, stem_weight, spatial_weight, temporal_weight, cotangent
):
    n = lax.axis_size("tile")
    nf = lax.axis_size("filt")
    n_slots, n_bands, cols = panels.shape
    n_dates, own, n_rows, _ = cotangent.shape
    chan = stem_weight.shape[1]
    bp = -(-24 // n)
    scale = 1.0 / math.sqrt(n_dates * n_rows * n * cols)
    weights = jnp.concatenate([spatial_weight.reshape(9, chan, own), temporal_weight], axis=0)
    wt = weights.transpose(2, 0, 1).reshape(own, 12 * chan)
    cot = cotangent.transpose(2, 0, 1, 3)
    dma = pltpu.SemaphoreType.DMA
    vmem = pl.BlockSpec(memory_space=pltpu.VMEM)
    smem = pl.BlockSpec(memory_space=pltpu.SMEM)
    out = pl.pallas_call(
        functools.partial(kernel, n, nf, bp, scale),
        out_shape=(
            jax.ShapeDtypeStruct((n_dates, n_rows, own, cols), BF16),
            jax.ShapeDtypeStruct((n_bands, chan), F32),
            jax.ShapeDtypeStruct((9, chan, own), F32),
            jax.ShapeDtypeStruct((3, chan, own), F32),
            jax.ShapeDtypeStruct((n_dates, n_bands, cols), F32),
        ),
        in_specs=[smem, smem, vmem, vmem, vmem, vmem],
        out_specs=(vmem,) * 5,
        scratch_shapes=[
            pltpu.VMEM((n_slots, 16, cols), F32),
            pltpu.VMEM((n, 32, cols), BF16),
            pltpu.VMEM((n, 32, cols), BF16),
            pltpu.VMEM((8, 32, cols), BF16),
            pltpu.VMEM((chan, 12 * chan), BF16),
            pltpu.VMEM((chan, 12 * chan), BF16),
            pltpu.VMEM((16, chan), BF16),
            pltpu.VMEM((cols, chan), F32),
            pltpu.VMEM((6, 2, chan, cols), BF16),
            pltpu.VMEM((3 * chan, 2 * 8 * cols), BF16),
            pltpu.VMEM((2 * chan, 4 * cols), BF16),
            pltpu.VMEM((chan, 2 * 6 * cols), BF16),
            pltpu.VMEM((3 * chan, 6 * cols), BF16),
            pltpu.VMEM((n, bp * 16, cols), BF16),
            pltpu.VMEM((n, bp * 16, cols), BF16),
            pltpu.VMEM((n, bp * 16, cols), BF16),
            pltpu.VMEM((16, cols), F32),
            pltpu.VMEM((nf, 16, cols), F32),
            pltpu.VMEM((16, cols), F32),
            pltpu.VMEM((n, 16, cols), F32),
            dma((n,)), dma((n,)), dma((8,)), dma((8,)), dma((nf,)), dma((nf,)),
            dma((nf,)), dma((nf,)), dma((nf,)), dma((nf,)), dma((nf,)), dma((nf,)),
            dma((n,)), dma((n,)), dma((n,)), dma((n,)), dma((nf,)), dma((nf,)), dma((n,)), dma((n,)),
        ],
        compiler_params=pltpu.CompilerParams(
            collective_id=0, has_side_effects=True, vmem_limit_bytes=40 * 1024 * 1024
        ),
    )(panel_tile, panel_date, panels, stem_weight, wt, cot)
    features_out, grad_stem, grad_spatial, grad_temporal, band_grad = out
    return (
        features_out.transpose(0, 2, 1, 3),
        grad_stem,
        grad_spatial.reshape(3, 3, chan, own),
        grad_temporal,
        band_grad,
    )


def solution(mesh):
    in_specs = (
        P("tile", None, "filt"),
        P("tile", None),
        P("tile"),
        P(),
        P(None, None, None, "filt"),
        P(None, None, "filt"),
        P(None, "filt", "tile", None),
    )
    out_specs = (
        P(None, "filt", "tile", None),
        P(),
        P(None, None, None, "filt"),
        P(None, None, "filt"),
        P(None, None, ("tile", "filt")),
    )
    return jax.shard_map(
        per_device, mesh=mesh, in_specs=in_specs, out_specs=out_specs, check_vma=False
    )
```

```python
import functools
import math

import jax
import jax.numpy as jnp
from jax import lax
from jax.experimental import pallas as pl
from jax.experimental.pallas import tpu as pltpu
from jax.sharding import PartitionSpec as P

MESH = pl.DeviceIdType.MESH
F32 = jnp.float32
BF16 = jnp.bfloat16


def loop(count, body):
    if count <= 8:
        for i in range(count):
            body(i)
    else:
        lax.fori_loop(0, count, lambda i, c: (body(i), c)[1], 0)


def total(count, term):
    if count <= 8:
        out = term(0)
        for i in range(1, count):
            out = out + term(i)
        return out
    return lax.fori_loop(1, count, lambda i, c: c + term(i), term(0))


def dot(a, b):
    return jnp.dot(a, b, preferred_element_type=F32)


def dot_t(a, b):
    return lax.dot_general(a, b, (((1,), (1,)), ((), ())), preferred_element_type=F32)


def shifted(block, offset):
    cols = block.shape[1]
    lane = lax.broadcasted_iota(jnp.int32, block.shape, 1)
    if offset == 1:
        return jnp.where(lane == cols - 1, 0.0, pltpu.roll(block, cols - 1, 1))
    return jnp.where(lane == 0, 0.0, pltpu.roll(block, 1, 1))


def kernel(
    n, nf, bp, scale,
    tile_ref, date_ref, panels_ref, stem_ref, ws_ref, wtm_ref, cot_ref,
    fo_ref, gstem_ref, grad_ref, bg_ref,
    pp, pan_out, pan_in, raw, wall, wback, stem16, stem_t, cot, feat, act, pre_g, pg3,
    rs_out, rs_in, ag, sa_out, sa, sb_out, sb,
    pan_s, pan_r, raw_s, raw_r, w_s, w_r, c_s, c_r, lo_s, lo_r, hi_s, hi_r,
    rs_s, rs_r, ag_s, ag_r, sa_s, sa_r, sb_s, sb_r,
):
    j = lax.axis_index("tile")
    f = lax.axis_index("filt")
    bands, n_slots = panels_ref.shape[0:2]
    own = ws_ref.shape[1]
    chan = own * nf
    cols = 128

    def tpeer(d):
        return lax.rem(j + d, n)

    def fpeer(d):
        return lax.rem(f + d, nf)

    def remote(src, dst, s, r, to):
        return pltpu.make_async_remote_copy(
            src_ref=src, dst_ref=dst, send_sem=s, recv_sem=r, device_id=to, device_id_type=MESH
        )

    barrier = pltpu.get_barrier_semaphore()

    def hello(t, g):
        pl.semaphore_signal(barrier, inc=1, device_id=(t, g), device_id_type=MESH)

    loop(n - 1, lambda d: hello(tpeer(d + 1), f))
    for d in range(1, nf):
        hello(j, fpeer(d))

    @pl.when(j > 0)
    def _():
        for d in range(1, nf):
            hello(j - 1, fpeer(d))

    @pl.when(j < n - 1)
    def _():
        for d in range(1, nf):
            hello(j + 1, fpeer(d))

    mine = pl.ds(pl.multiple_of(f * own, own), own)
    for q in range(12):
        wall[mine, q * chan : (q + 1) * chan] = ws_ref[q] if q < 9 else wtm_ref[q - 9]
    pad_rows = lax.broadcasted_iota(jnp.int32, (n_slots, 16, cols), 1)
    pp[...] = jnp.where(pad_rows == bands, 1.0, 0.0)
    for b in range(bands):
        pp[:, b, :] = panels_ref[b].astype(F32)

    def fill(k):
        def term(s):
            block = pp[s]
            here = tile_ref[0, s] == k
            first = jnp.where(here & (date_ref[s] == 0), 1.0, 0.0)
            second = jnp.where(here & (date_ref[s] == 1), 1.0, 0.0)
            return jnp.concatenate([block * first, block * second], axis=0)

        pan_out[k] = total(n_slots, term).astype(BF16)

    loop(n, fill)

    @pl.when(j == 0)
    def _():
        raw[0:2] = jnp.zeros((2, 32, cols), BF16)
        cot[0] = jnp.zeros((2, chan, cols), BF16)

    @pl.when(j == n - 1)
    def _():
        raw[6:8] = jnp.zeros((2, 32, cols), BF16)
        cot[5] = jnp.zeros((2, chan, cols), BF16)

    sides = jnp.where(j > 0, 1, 0) + jnp.where(j < n - 1, 1, 0)
    pl.semaphore_wait(barrier, n - 1 + (nf - 1) * (1 + sides))

    def pan_copy(d):
        k = tpeer(d)
        return remote(pan_out.at[k], pan_in.at[j], pan_s.at[d], pan_r.at[j], (k, f))

    def pan_wait(d):
        k = tpeer(d)
        remote(pan_out.at[k], pan_in.at[k], pan_s.at[d], pan_r.at[k], (k, f)).wait_recv()

    loop(n - 1, lambda d: pan_copy(d + 1).start())

    sib = f + 1 - 2 * lax.rem(f, 2)
    par = lax.rem(f + 2, nf)
    diag = lax.rem(sib + 2, nf)

    def group(g):
        return pl.ds(pl.multiple_of(g * own, own), own)

    def w_copy(to, slot):
        return remote(wall.at[mine], wall.at[mine], w_s.at[slot], w_r.at[f], (j, to))

    def c_copy(to, slot):
        return remote(cot_ref, cot.at[pl.ds(1, 4), :, mine, :], c_s.at[slot], c_r.at[f], (j, to))

    def w_forward():
        at = wall.at[group(par)]
        return remote(at, at, w_s.at[2], w_r.at[par], (j, sib))

    def c_forward():
        at = cot.at[pl.ds(1, 4), :, group(par), :]
        return remote(at, at, c_s.at[2], c_r.at[par], (j, sib))

    def w_wait(g):
        remote(wall.at[mine], wall.at[group(g)], w_s.at[0], w_r.at[g], (j, par)).wait_recv()

    def c_wait(g):
        at = cot.at[pl.ds(1, 4), :, group(g), :]
        remote(cot_ref, at, c_s.at[0], c_r.at[g], (j, par)).wait_recv()

    def lo_copy(d):
        return remote(cot_ref.at[3], cot.at[0, :, mine, :], lo_s.at[d], lo_r.at[f], (j + 1, fpeer(d)))

    def hi_copy(d):
        return remote(cot_ref.at[0], cot.at[5, :, mine, :], hi_s.at[d], hi_r.at[f], (j - 1, fpeer(d)))

    w_copy(par, 0).start()
    w_copy(sib, 1).start()
    c_copy(par, 0).start()
    c_copy(sib, 1).start()

    @pl.when(j < n - 1)
    def _():
        for d in range(nf):
            lo_copy(d).start()

    @pl.when(j > 0)
    def _():
        for d in range(nf):
            hi_copy(d).start()

    cot[1:5, :, mine, :] = cot_ref[...]
    stem_t[...] = jnp.zeros((cols, chan), F32)
    stem_t[0:bands, :] = stem_ref[...].astype(F32)
    stem16[...] = stem_t[0:16, :].astype(BF16)
    stem_lhs = stem_t[...].T[:, 0:16].astype(BF16)

    pan_in[j] = pan_out[j]
    loop(n - 1, lambda d: pan_wait(d + 1))
    sums = total(n, lambda k: pan_in[k].astype(F32))
    row = jnp.concatenate(
        [
            sums[t * 16 : t * 16 + 16] / jnp.maximum(sums[t * 16 + bands : t * 16 + bands + 1], 1.0)
            for t in range(2)
        ],
        axis=0,
    ).astype(BF16)
    raw[2 + f] = row

    def raw_copy(d):
        return remote(raw.at[2 + f], raw.at[2 + f], raw_s.at[d], raw_r.at[2 + f], (j, fpeer(d)))

    def raw_down(d):
        return remote(raw.at[2 + f], raw.at[f - 2], raw_s.at[4 + d], raw_r.at[f - 2], (j + 1, fpeer(d)))

    def raw_up(d):
        return remote(raw.at[2 + f], raw.at[6 + f], raw_s.at[4 + d], raw_r.at[6 + f], (j - 1, fpeer(d)))

    for d in range(1, nf):
        raw_copy(d).start()
    goes_down = (f >= 2) & (j < n - 1)
    goes_up = (f < 2) & (j > 0)

    @pl.when(goes_down)
    def _():
        for d in range(nf):
            raw_down(d).start()

    @pl.when(goes_up)
    def _():
        for d in range(nf):
            raw_up(d).start()

    w_wait(par)
    w_forward().start()

    def raw_wait(slot):
        remote(raw.at[slot], raw.at[slot], raw_s.at[0], raw_r.at[slot], (j, fpeer(1))).wait_recv()

    for d in range(1, nf):
        raw_wait(2 + fpeer(d))

    @pl.when(j > 0)
    def _():
        raw_wait(0)
        raw_wait(1)

    @pl.when(j < n - 1)
    def _():
        raw_wait(6)
        raw_wait(7)

    for t in range(2):
        for r in range(8):
            block = dot(stem_lhs, raw[r, t * 16 : t * 16 + 16, :]).astype(BF16)
            at = (t * 8 + r) * cols
            wide = block.astype(F32)
            feat[0:chan, at : at + cols] = shifted(wide, -1).astype(BF16)
            feat[chan : 2 * chan, at : at + cols] = block
            feat[2 * chan : 3 * chan, at : at + cols] = shifted(wide, 1).astype(BF16)

    c_wait(par)
    c_forward().start()
    w_wait(sib)
    w_wait(diag)
    for q in range(12):
        block = wall[:, q * chan : (q + 1) * chan].astype(F32).T.astype(BF16)
        at = q if q < 9 else 9 + (11 - q)
        wback[:, at * chan : (at + 1) * chan] = block
    c_wait(sib)
    c_wait(diag)

    @pl.when(j > 0)
    def _():
        for g in range(nf):
            remote(cot_ref.at[3], cot.at[0, :, g * own : (g + 1) * own, :], lo_s.at[g], lo_r.at[g], (j - 1, g)).wait_recv()

    @pl.when(j < n - 1)
    def _():
        for g in range(nf):
            remote(cot_ref.at[0], cot.at[5, :, g * own : (g + 1) * own, :], hi_s.at[g], hi_r.at[g], (j + 1, g)).wait_recv()

    cot_rows = jnp.concatenate([cot[r].reshape(2 * chan, cols) for r in range(6)], axis=1)
    lane = lax.broadcasted_iota(jnp.int32, (chan, 6 * cols), 1)
    inside = ((lane >= cols) | (j > 0)) & ((lane < 5 * cols) | (j < n - 1))
    for t in range(2):
        pre = dot(wall[:, 0 : 3 * chan], feat[:, t * 1024 : t * 1024 + 768])
        for dy in (1, 2):
            at = t * 1024 + dy * cols
            pre = pre + dot(wall[:, dy * 3 * chan : (dy + 1) * 3 * chan], feat[:, at : at + 768])
        sigma = jax.nn.sigmoid(pre)
        act[t * chan : (t + 1) * chan, :] = (pre * sigma)[:, cols : 5 * cols].astype(BF16)
        act_grad = dot(wback[:, (10 - t) * chan : (12 - t) * chan], cot_rows)
        slope = sigma * (1.0 + pre * (1.0 - sigma))
        pre_g[:, t * 768 : (t + 1) * 768] = jnp.where(inside, act_grad * slope, 0.0).astype(BF16)

    def put(q, grad):
        for h in range(2):
            b = q * 2 + h
            rs_out[b // bp, (b % bp) * 16 : (b % bp) * 16 + 16, :] = grad[h * 16 : h * 16 + 16].astype(BF16)

    cot_own = [
        jnp.concatenate([cot_ref[r, t] for r in range(4)], axis=1) for t in range(2)
    ]
    act0, act1 = act[0:chan, :], act[chan : 2 * chan, :]
    put(9, dot_t(cot_own[1], act0) * scale)
    put(10, (dot_t(cot_own[0], act0) + dot_t(cot_own[1], act1)) * scale)
    put(11, dot_t(cot_own[0], act1) * scale)
    pg_own = [pre_g[mine, t * 768 + cols : t * 768 + 5 * cols] for t in range(2)]
    for dy in range(3):
        at = (dy + 1) * cols
        grad = dot_t(pg_own[0], feat[:, at : at + 512])
        grad = grad + dot_t(pg_own[1], feat[:, 1024 + at : 1024 + at + 512])
        grad = grad * scale
        for dx in range(3):
            put(dy * 3 + dx, grad[:, dx * chan : (dx + 1) * chan])
    if n * bp > 24:
        used = -(-24 // bp)
        loop(n - used, lambda k: rs_out.__setitem__(used + k, jnp.zeros((bp * 16, cols), BF16)))

    def rs_copy(d):
        k = tpeer(d)
        return remote(rs_out.at[k], rs_in.at[j], rs_s.at[d], rs_r.at[j], (k, f))

    loop(n - 1, lambda d: rs_copy(d + 1).start())
    rs_in[j] = rs_out[j]

    for t in range(2):
        for r in range(3):
            at = pl.ds(pl.multiple_of(t * 768 + (f + r) * cols, cols), cols)
            block = pre_g[:, at]
            wide = block.astype(F32)
            to = (r * 2 + t) * cols
            pg3[0:chan, to : to + cols] = shifted(wide, 1).astype(BF16)
            pg3[chan : 2 * chan, to : to + cols] = block
            pg3[2 * chan : 3 * chan, to : to + cols] = shifted(wide, -1).astype(BF16)
    fgrad = jnp.concatenate([cot[1 + f, t].astype(F32) for t in range(2)], axis=1)
    for dy in range(3):
        at = (2 - dy) * 2 * cols
        fgrad = fgrad + dot(wback[:, dy * 3 * chan : (dy + 1) * 3 * chan], pg3[:, at : at + 2 * cols])
    upper = fgrad.astype(BF16)
    lower = (fgrad - upper.astype(F32)).astype(BF16)
    own_raw = raw[2 + f]
    raw_row = jnp.concatenate([own_raw[0:16], own_raw[16:32]], axis=1)
    sa_out[...] = (dot_t(raw_row, upper) + dot_t(raw_row, lower)) * scale

    def sa_copy(d):
        return remote(sa_out, sa.at[f], sa_s.at[d], sa_r.at[f], (j, fpeer(d)))

    for d in range(1, nf):
        sa_copy(d).start()
    sa[f] = sa_out[...]
    bgrad = dot(stem16[...], upper) + dot(stem16[...], lower)
    for t in range(2):
        bg_ref[t] = bgrad[0:bands, t * cols : (t + 1) * cols]

    wt_time = wall[mine, 9 * chan : 12 * chan]
    feat_own = pl.ds(pl.multiple_of(chan + f * own, own), own)
    for t in range(2):
        out = dot(wt_time[:, (1 - t) * chan : (3 - t) * chan], act[...])
        out = out + feat[feat_own, t * 1024 + 256 : t * 1024 + 768].astype(F32)
        for r in range(4):
            fo_ref[t, r] = out[:, r * cols : (r + 1) * cols].astype(BF16)

    for d in range(1, nf):
        g = fpeer(d)
        remote(sa_out, sa.at[g], sa_s.at[d], sa_r.at[g], (j, g)).wait_recv()
    sb_out[...] = (sa[0] + sa[1]) + (sa[2] + sa[3])

    def sb_copy(d):
        k = tpeer(d)
        return remote(sb_out, sb.at[j], sb_s.at[d], sb_r.at[j], (k, f))

    loop(n - 1, lambda d: sb_copy(d + 1).start())
    sb[j] = sb_out[...]

    def rs_wait(d):
        k = tpeer(d)
        remote(rs_out.at[k], rs_in.at[k], rs_s.at[d], rs_r.at[k], (k, f)).wait_recv()

    loop(n - 1, lambda d: rs_wait(d + 1))
    ag[j] = total(n, lambda k: rs_in[k].astype(F32)).astype(BF16)

    def ag_copy(d):
        k = tpeer(d)
        return remote(ag.at[j], ag.at[j], ag_s.at[d], ag_r.at[j], (k, f))

    loop(n - 1, lambda d: ag_copy(d + 1).start())

    w_copy(par, 0).wait_send()
    w_copy(sib, 1).wait_send()
    w_forward().wait_send()
    c_copy(par, 0).wait_send()
    c_copy(sib, 1).wait_send()
    c_forward().wait_send()
    loop(n - 1, lambda d: pan_copy(d + 1).wait_send())
    for d in range(1, nf):
        raw_copy(d).wait_send()
        sa_copy(d).wait_send()

    @pl.when(j < n - 1)
    def _():
        for d in range(nf):
            lo_copy(d).wait_send()

    @pl.when(j > 0)
    def _():
        for d in range(nf):
            hi_copy(d).wait_send()

    @pl.when(goes_down)
    def _():
        for d in range(nf):
            raw_down(d).wait_send()

    @pl.when(goes_up)
    def _():
        for d in range(nf):
            raw_up(d).wait_send()

    loop(n - 1, lambda d: rs_copy(d + 1).wait_send())

    def sb_wait(d):
        k = tpeer(d)
        remote(sb_out, sb.at[k], sb_s.at[d], sb_r.at[k], (k, f)).wait_recv()

    loop(n - 1, lambda d: sb_wait(d + 1))
    gstem_ref[...] = total(n, lambda k: sb[k])[0:bands]

    def ag_wait(d):
        k = tpeer(d)
        remote(ag.at[k], ag.at[k], ag_s.at[d], ag_r.at[k], (k, f)).wait_recv()

    loop(n - 1, lambda d: ag_wait(d + 1))
    for b in range(24):
        grad_ref[b] = ag[b // bp, (b % bp) * 16 : (b % bp) * 16 + 16, :]
    loop(n - 1, lambda d: ag_copy(d + 1).wait_send())
    loop(n - 1, lambda d: sb_copy(d + 1).wait_send())


def finish(fo_in, gstem_in, grad_in, bg_in, fo_ref, gstem_ref, gsp_ref, gtm_ref, bg_ref):
    for t in range(2):
        fo_ref[t] = jnp.swapaxes(fo_in[t].astype(F32), 0, 1).astype(BF16)
    gstem_ref[...] = gstem_in[...]
    for t in range(2):
        bg_ref[:, t, :] = bg_in[t]
    for q in range(12):
        for h in range(2):
            block = grad_in[2 * q + h].astype(F32)
            if q < 9:
                gsp_ref[q, h * 16 : h * 16 + 16, :] = block
            else:
                gtm_ref[q - 9, h * 16 : h * 16 + 16, :] = block


def per_device(
    panels, panel_tile, panel_date, stem_weight, spatial_weight, temporal_weight, cotangent
):
    n = lax.axis_size("tile")
    nf = lax.axis_size("filt")
    n_slots, n_bands, cols = panels.shape
    n_dates, own, n_rows, _ = cotangent.shape
    chan = stem_weight.shape[1]
    bp = -(-24 // n)
    scale = 1.0 / math.sqrt(n_dates * n_rows * n * cols)
    ws = spatial_weight.transpose(0, 1, 3, 2).reshape(9, own, chan)
    wtm = temporal_weight.transpose(0, 2, 1)
    cot = cotangent.transpose(2, 0, 1, 3)
    dma = pltpu.SemaphoreType.DMA
    vmem = pl.BlockSpec(memory_space=pltpu.VMEM)
    smem = pl.BlockSpec(memory_space=pltpu.SMEM)
    out = pl.pallas_call(
        functools.partial(kernel, n, nf, bp, scale),
        out_shape=(
            jax.ShapeDtypeStruct((n_dates, n_rows, own, cols), BF16),
            jax.ShapeDtypeStruct((n_bands, chan), F32),
            jax.ShapeDtypeStruct((24, 16, cols), BF16),
            jax.ShapeDtypeStruct((n_dates, n_bands, cols), F32),
        ),
        in_specs=[smem, smem, vmem, vmem, vmem, vmem, vmem],
        out_specs=(vmem,) * 4,
        scratch_shapes=[
            pltpu.VMEM((n_slots, 16, cols), F32),
            pltpu.VMEM((n, 32, cols), BF16),
            pltpu.VMEM((n, 32, cols), BF16),
            pltpu.VMEM((8, 32, cols), BF16),
            pltpu.VMEM((chan, 12 * chan), BF16),
            pltpu.VMEM((chan, 12 * chan), BF16),
            pltpu.VMEM((16, chan), BF16),
            pltpu.VMEM((cols, chan), F32),
            pltpu.VMEM((6, 2, chan, cols), BF16),
            pltpu.VMEM((3 * chan, 2 * 8 * cols), BF16),
            pltpu.VMEM((2 * chan, 4 * cols), BF16),
            pltpu.VMEM((chan, 2 * 6 * cols), BF16),
            pltpu.VMEM((3 * chan, 6 * cols), BF16),
            pltpu.VMEM((n, bp * 16, cols), BF16),
            pltpu.VMEM((n, bp * 16, cols), BF16),
            pltpu.VMEM((n, bp * 16, cols), BF16),
            pltpu.VMEM((16, cols), F32),
            pltpu.VMEM((nf, 16, cols), F32),
            pltpu.VMEM((16, cols), F32),
            pltpu.VMEM((n, 16, cols), F32),
            dma((n,)), dma((n,)), dma((8,)), dma((8,)), dma((nf,)), dma((nf,)),
            dma((nf,)), dma((nf,)), dma((nf,)), dma((nf,)), dma((nf,)), dma((nf,)),
            dma((n,)), dma((n,)), dma((n,)), dma((n,)), dma((nf,)), dma((nf,)), dma((n,)), dma((n,)),
        ],
        compiler_params=pltpu.CompilerParams(
            collective_id=0, has_side_effects=True, vmem_limit_bytes=40 * 1024 * 1024
        ),
    )(panel_tile.T, panel_date, panels.transpose(1, 0, 2), stem_weight, ws, wtm, cot)
    features_out, grad_stem, gsp, gtm, bg = pl.pallas_call(
        finish,
        out_shape=(
            jax.ShapeDtypeStruct((n_dates, own, n_rows, cols), BF16),
            jax.ShapeDtypeStruct((n_bands, chan), F32),
            jax.ShapeDtypeStruct((9, own, chan), F32),
            jax.ShapeDtypeStruct((3, own, chan), F32),
            jax.ShapeDtypeStruct((n_bands, n_dates, cols), F32),
        ),
        in_specs=[vmem] * 4,
        out_specs=(vmem,) * 5,
    )(*out)
    return (
        features_out,
        grad_stem,
        gsp.reshape(3, 3, own, chan).transpose(0, 1, 3, 2),
        gtm.transpose(0, 2, 1),
        bg.transpose(1, 0, 2),
    )


def solution(mesh):
    in_specs = (
        P("tile", None, "filt"),
        P("tile", None),
        P("tile"),
        P(),
        P(None, None, None, "filt"),
        P(None, None, "filt"),
        P(None, "filt", "tile", None),
    )
    out_specs = (
        P(None, "filt", "tile", None),
        P(),
        P(None, None, None, "filt"),
        P(None, None, "filt"),
        P(None, None, ("tile", "filt")),
    )
    return jax.shard_map(
        per_device, mesh=mesh, in_specs=in_specs, out_specs=out_specs, check_vma=False
    )
```

```python
import functools
import math

import jax
import jax.numpy as jnp
from jax import lax
from jax.experimental import pallas as pl
from jax.experimental.pallas import tpu as pltpu
from jax.sharding import PartitionSpec as P

MESH = pl.DeviceIdType.MESH
F32 = jnp.float32
BF16 = jnp.bfloat16


def loop(count, body):
    if count <= 8:
        for i in range(count):
            body(i)
    else:
        lax.fori_loop(0, count, lambda i, c: (body(i), c)[1], 0)


def total(count, term):
    if count <= 8:
        out = term(0)
        for i in range(1, count):
            out = out + term(i)
        return out
    return lax.fori_loop(1, count, lambda i, c: c + term(i), term(0))


def dot(a, b):
    return jnp.dot(a, b, preferred_element_type=F32)


def dot_t(a, b):
    return lax.dot_general(a, b, (((1,), (1,)), ((), ())), preferred_element_type=F32)


def shifted(block, offset):
    cols = block.shape[1]
    lane = lax.broadcasted_iota(jnp.int32, block.shape, 1)
    if offset == 1:
        return jnp.where(lane == cols - 1, 0.0, pltpu.roll(block, cols - 1, 1))
    return jnp.where(lane == 0, 0.0, pltpu.roll(block, 1, 1))


def kernel(
    n, nf, bp, scale,
    tile_ref, date_ref, panels_ref, stem_ref, ws_ref, wtm_ref, cot_ref,
    res_ref,
    pp, pan_out, pan_in, raw, wall, wback, stem16, stem_t, cot, feat, act, pre_g, pg3,
    rs_out, rs_in, ag, sa_out, sa, sb_out, sb,
    pan_s, pan_r, raw_s, raw_r, w_s, w_r, c_s, c_r, lo_s, lo_r, hi_s, hi_r,
    rs_s, rs_r, ag_s, ag_r, sa_s, sa_r, sb_s, sb_r,
):
    j = lax.axis_index("tile")
    f = lax.axis_index("filt")
    bands, n_slots = panels_ref.shape[0:2]
    own = ws_ref.shape[1]
    chan = own * nf
    cols = 128

    def tpeer(d):
        return lax.rem(j + d, n)

    def fpeer(d):
        return lax.rem(f + d, nf)

    def remote(src, dst, s, r, to):
        return pltpu.make_async_remote_copy(
            src_ref=src, dst_ref=dst, send_sem=s, recv_sem=r, device_id=to, device_id_type=MESH
        )

    barrier = pltpu.get_barrier_semaphore()

    def hello(t, g):
        pl.semaphore_signal(barrier, inc=1, device_id=(t, g), device_id_type=MESH)

    loop(n - 1, lambda d: hello(tpeer(d + 1), f))
    for d in range(1, nf):
        hello(j, fpeer(d))

    @pl.when(j > 0)
    def _():
        for d in range(1, nf):
            hello(j - 1, fpeer(d))

    @pl.when(j < n - 1)
    def _():
        for d in range(1, nf):
            hello(j + 1, fpeer(d))

    mine = pl.ds(pl.multiple_of(f * own, own), own)
    for q in range(12):
        wall[mine, q * chan : (q + 1) * chan] = ws_ref[q] if q < 9 else wtm_ref[q - 9]
    for t in range(2):
        for r in range(4):
            cot[1 + r, t, mine, :] = cot_ref[r, t]
    pad_rows = lax.broadcasted_iota(jnp.int32, (n_slots, 16, cols), 1)
    pp[...] = jnp.where(pad_rows == bands, 1.0, 0.0)
    for b in range(bands):
        pp[:, b, :] = panels_ref[b].astype(F32)

    def fill(k):
        def term(s):
            block = pp[s]
            here = tile_ref[0, s] == k
            first = jnp.where(here & (date_ref[s] == 0), 1.0, 0.0)
            second = jnp.where(here & (date_ref[s] == 1), 1.0, 0.0)
            return jnp.concatenate([block * first, block * second], axis=0)

        pan_out[k] = total(n_slots, term).astype(BF16)

    loop(n, fill)

    @pl.when(j == 0)
    def _():
        raw[0:2] = jnp.zeros((2, 32, cols), BF16)
        cot[0] = jnp.zeros((2, chan, cols), BF16)

    @pl.when(j == n - 1)
    def _():
        raw[6:8] = jnp.zeros((2, 32, cols), BF16)
        cot[5] = jnp.zeros((2, chan, cols), BF16)

    sides = jnp.where(j > 0, 1, 0) + jnp.where(j < n - 1, 1, 0)
    pl.semaphore_wait(barrier, n - 1 + (nf - 1) * (1 + sides))

    def pan_copy(d):
        k = tpeer(d)
        return remote(pan_out.at[k], pan_in.at[j], pan_s.at[d], pan_r.at[j], (k, f))

    def pan_wait(d):
        k = tpeer(d)
        remote(pan_out.at[k], pan_in.at[k], pan_s.at[d], pan_r.at[k], (k, f)).wait_recv()

    loop(n - 1, lambda d: pan_copy(d + 1).start())

    sib = f + 1 - 2 * lax.rem(f, 2)
    par = lax.rem(f + 2, nf)
    diag = lax.rem(sib + 2, nf)

    def group(g):
        return pl.ds(pl.multiple_of(g * own, own), own)

    def w_copy(to, slot):
        return remote(wall.at[mine], wall.at[mine], w_s.at[slot], w_r.at[f], (j, to))

    def c_copy(to, slot):
        return remote(cot.at[pl.ds(1, 4), :, mine, :], cot.at[pl.ds(1, 4), :, mine, :], c_s.at[slot], c_r.at[f], (j, to))

    def w_forward():
        at = wall.at[group(par)]
        return remote(at, at, w_s.at[2], w_r.at[par], (j, sib))

    def c_forward():
        at = cot.at[pl.ds(1, 4), :, group(par), :]
        return remote(at, at, c_s.at[2], c_r.at[par], (j, sib))

    def w_wait(g):
        remote(wall.at[mine], wall.at[group(g)], w_s.at[0], w_r.at[g], (j, par)).wait_recv()

    def c_wait(g):
        at = cot.at[pl.ds(1, 4), :, group(g), :]
        remote(cot.at[pl.ds(1, 4), :, mine, :], at, c_s.at[0], c_r.at[g], (j, par)).wait_recv()

    def lo_copy(d):
        return remote(cot.at[4, :, mine, :], cot.at[0, :, mine, :], lo_s.at[d], lo_r.at[f], (j + 1, fpeer(d)))

    def hi_copy(d):
        return remote(cot.at[1, :, mine, :], cot.at[5, :, mine, :], hi_s.at[d], hi_r.at[f], (j - 1, fpeer(d)))

    w_copy(par, 0).start()
    w_copy(sib, 1).start()
    c_copy(par, 0).start()
    c_copy(sib, 1).start()

    @pl.when(j < n - 1)
    def _():
        for d in range(nf):
            lo_copy(d).start()

    @pl.when(j > 0)
    def _():
        for d in range(nf):
            hi_copy(d).start()

    stem_t[...] = jnp.zeros((cols, chan), F32)
    stem_t[0:bands, :] = stem_ref[...].astype(F32)
    stem16[...] = stem_t[0:16, :].astype(BF16)
    stem_lhs = stem_t[...].T[:, 0:16].astype(BF16)

    pan_in[j] = pan_out[j]
    loop(n - 1, lambda d: pan_wait(d + 1))
    sums = total(n, lambda k: pan_in[k].astype(F32))
    row = jnp.concatenate(
        [
            sums[t * 16 : t * 16 + 16] / jnp.maximum(sums[t * 16 + bands : t * 16 + bands + 1], 1.0)
            for t in range(2)
        ],
        axis=0,
    ).astype(BF16)
    raw[2 + f] = row

    def raw_copy(d):
        return remote(raw.at[2 + f], raw.at[2 + f], raw_s.at[d], raw_r.at[2 + f], (j, fpeer(d)))

    def raw_down(d):
        return remote(raw.at[2 + f], raw.at[f - 2], raw_s.at[4 + d], raw_r.at[f - 2], (j + 1, fpeer(d)))

    def raw_up(d):
        return remote(raw.at[2 + f], raw.at[6 + f], raw_s.at[4 + d], raw_r.at[6 + f], (j - 1, fpeer(d)))

    for d in range(1, nf):
        raw_copy(d).start()
    goes_down = (f >= 2) & (j < n - 1)
    goes_up = (f < 2) & (j > 0)

    @pl.when(goes_down)
    def _():
        for d in range(nf):
            raw_down(d).start()

    @pl.when(goes_up)
    def _():
        for d in range(nf):
            raw_up(d).start()

    w_wait(par)
    w_forward().start()

    def raw_wait(slot):
        remote(raw.at[slot], raw.at[slot], raw_s.at[0], raw_r.at[slot], (j, fpeer(1))).wait_recv()

    for d in range(1, nf):
        raw_wait(2 + fpeer(d))

    @pl.when(j > 0)
    def _():
        raw_wait(0)
        raw_wait(1)

    @pl.when(j < n - 1)
    def _():
        raw_wait(6)
        raw_wait(7)

    for t in range(2):
        for r in range(8):
            block = dot(stem_lhs, raw[r, t * 16 : t * 16 + 16, :]).astype(BF16)
            at = (t * 8 + r) * cols
            wide = block.astype(F32)
            feat[0:chan, at : at + cols] = shifted(wide, -1).astype(BF16)
            feat[chan : 2 * chan, at : at + cols] = block
            feat[2 * chan : 3 * chan, at : at + cols] = shifted(wide, 1).astype(BF16)

    c_wait(par)
    c_forward().start()
    w_wait(sib)
    w_wait(diag)
    for q in range(12):
        block = wall[:, q * chan : (q + 1) * chan].astype(F32).T.astype(BF16)
        at = q if q < 9 else 9 + (11 - q)
        wback[:, at * chan : (at + 1) * chan] = block
    c_wait(sib)
    c_wait(diag)

    @pl.when(j > 0)
    def _():
        for g in range(nf):
            remote(cot.at[4, :, mine, :], cot.at[0, :, g * own : (g + 1) * own, :], lo_s.at[g], lo_r.at[g], (j - 1, g)).wait_recv()

    @pl.when(j < n - 1)
    def _():
        for g in range(nf):
            remote(cot.at[1, :, mine, :], cot.at[5, :, g * own : (g + 1) * own, :], hi_s.at[g], hi_r.at[g], (j + 1, g)).wait_recv()

    cot_rows = jnp.concatenate([cot[r].reshape(2 * chan, cols) for r in range(6)], axis=1)
    lane = lax.broadcasted_iota(jnp.int32, (chan, 6 * cols), 1)
    inside = ((lane >= cols) | (j > 0)) & ((lane < 5 * cols) | (j < n - 1))
    for t in range(2):
        pre = dot(wall[:, 0 : 3 * chan], feat[:, t * 1024 : t * 1024 + 768])
        for dy in (1, 2):
            at = t * 1024 + dy * cols
            pre = pre + dot(wall[:, dy * 3 * chan : (dy + 1) * 3 * chan], feat[:, at : at + 768])
        sigma = jax.nn.sigmoid(pre)
        act[t * chan : (t + 1) * chan, :] = (pre * sigma)[:, cols : 5 * cols].astype(BF16)
        act_grad = dot(wback[:, (10 - t) * chan : (12 - t) * chan], cot_rows)
        slope = sigma * (1.0 + pre * (1.0 - sigma))
        pre_g[:, t * 768 : (t + 1) * 768] = jnp.where(inside, act_grad * slope, 0.0).astype(BF16)

    def put(q, grad):
        for h in range(2):
            b = q * 2 + h
            rs_out[b // bp, (b % bp) * 16 : (b % bp) * 16 + 16, :] = grad[h * 16 : h * 16 + 16].astype(BF16)

    cot_own = [
        jnp.concatenate([cot[1 + r, t, mine, :] for r in range(4)], axis=1) for t in range(2)
    ]
    act0, act1 = act[0:chan, :], act[chan : 2 * chan, :]
    put(9, dot_t(cot_own[1], act0) * scale)
    put(10, (dot_t(cot_own[0], act0) + dot_t(cot_own[1], act1)) * scale)
    put(11, dot_t(cot_own[0], act1) * scale)
    pg_own = [pre_g[mine, t * 768 + cols : t * 768 + 5 * cols] for t in range(2)]
    for dy in range(3):
        at = (dy + 1) * cols
        grad = dot_t(pg_own[0], feat[:, at : at + 512])
        grad = grad + dot_t(pg_own[1], feat[:, 1024 + at : 1024 + at + 512])
        grad = grad * scale
        for dx in range(3):
            put(dy * 3 + dx, grad[:, dx * chan : (dx + 1) * chan])
    if n * bp > 24:
        used = -(-24 // bp)
        loop(n - used, lambda k: rs_out.__setitem__(used + k, jnp.zeros((bp * 16, cols), BF16)))

    def rs_copy(d):
        k = tpeer(d)
        return remote(rs_out.at[k], rs_in.at[j], rs_s.at[d], rs_r.at[j], (k, f))

    loop(n - 1, lambda d: rs_copy(d + 1).start())
    rs_in[j] = rs_out[j]

    for t in range(2):
        for r in range(3):
            at = pl.ds(pl.multiple_of(t * 768 + (f + r) * cols, cols), cols)
            block = pre_g[:, at]
            wide = block.astype(F32)
            to = (r * 2 + t) * cols
            pg3[0:chan, to : to + cols] = shifted(wide, 1).astype(BF16)
            pg3[chan : 2 * chan, to : to + cols] = block
            pg3[2 * chan : 3 * chan, to : to + cols] = shifted(wide, -1).astype(BF16)
    fgrad = jnp.concatenate([cot[1 + f, t].astype(F32) for t in range(2)], axis=1)
    for dy in range(3):
        at = (2 - dy) * 2 * cols
        fgrad = fgrad + dot(wback[:, dy * 3 * chan : (dy + 1) * 3 * chan], pg3[:, at : at + 2 * cols])
    upper = fgrad.astype(BF16)
    lower = (fgrad - upper.astype(F32)).astype(BF16)
    own_raw = raw[2 + f]
    raw_row = jnp.concatenate([own_raw[0:16], own_raw[16:32]], axis=1)
    sa_out[...] = (dot_t(raw_row, upper) + dot_t(raw_row, lower)) * scale

    def sa_copy(d):
        return remote(sa_out, sa.at[f], sa_s.at[d], sa_r.at[f], (j, fpeer(d)))

    for d in range(1, nf):
        sa_copy(d).start()
    sa[f] = sa_out[...]
    bgrad = dot(stem16[...], upper) + dot(stem16[...], lower)
    for t in range(2):
        res_ref[656 + t * 16 : 672 + t * 16, :] = bgrad[:, t * cols : (t + 1) * cols]

    wt_time = wall[mine, 9 * chan : 12 * chan]
    feat_own = pl.ds(pl.multiple_of(chan + f * own, own), own)
    for t in range(2):
        out = dot(wt_time[:, (1 - t) * chan : (3 - t) * chan], act[...])
        out = out + feat[feat_own, t * 1024 + 256 : t * 1024 + 768].astype(F32)
        for r in range(4):
            at = (t * 4 + r) * own
            res_ref[at : at + own, :] = out[:, r * cols : (r + 1) * cols]

    for d in range(1, nf):
        g = fpeer(d)
        remote(sa_out, sa.at[g], sa_s.at[d], sa_r.at[g], (j, g)).wait_recv()
    sb_out[...] = (sa[0] + sa[1]) + (sa[2] + sa[3])

    def sb_copy(d):
        k = tpeer(d)
        return remote(sb_out, sb.at[j], sb_s.at[d], sb_r.at[j], (k, f))

    loop(n - 1, lambda d: sb_copy(d + 1).start())
    sb[j] = sb_out[...]

    def rs_wait(d):
        k = tpeer(d)
        remote(rs_out.at[k], rs_in.at[k], rs_s.at[d], rs_r.at[k], (k, f)).wait_recv()

    loop(n - 1, lambda d: rs_wait(d + 1))
    ag[j] = total(n, lambda k: rs_in[k].astype(F32)).astype(BF16)

    def ag_copy(d):
        k = tpeer(d)
        return remote(ag.at[j], ag.at[j], ag_s.at[d], ag_r.at[j], (k, f))

    loop(n - 1, lambda d: ag_copy(d + 1).start())

    w_copy(par, 0).wait_send()
    w_copy(sib, 1).wait_send()
    w_forward().wait_send()
    c_copy(par, 0).wait_send()
    c_copy(sib, 1).wait_send()
    c_forward().wait_send()
    loop(n - 1, lambda d: pan_copy(d + 1).wait_send())
    for d in range(1, nf):
        raw_copy(d).wait_send()
        sa_copy(d).wait_send()

    @pl.when(j < n - 1)
    def _():
        for d in range(nf):
            lo_copy(d).wait_send()

    @pl.when(j > 0)
    def _():
        for d in range(nf):
            hi_copy(d).wait_send()

    @pl.when(goes_down)
    def _():
        for d in range(nf):
            raw_down(d).wait_send()

    @pl.when(goes_up)
    def _():
        for d in range(nf):
            raw_up(d).wait_send()

    loop(n - 1, lambda d: rs_copy(d + 1).wait_send())

    def sb_wait(d):
        k = tpeer(d)
        remote(sb_out, sb.at[k], sb_s.at[d], sb_r.at[k], (k, f)).wait_recv()

    loop(n - 1, lambda d: sb_wait(d + 1))
    res_ref[640:656, :] = total(n, lambda k: sb[k])

    def ag_wait(d):
        k = tpeer(d)
        remote(ag.at[k], ag.at[k], ag_s.at[d], ag_r.at[k], (k, f)).wait_recv()

    loop(n - 1, lambda d: ag_wait(d + 1))
    for b in range(24):
        block = ag[b // bp, (b % bp) * 16 : (b % bp) * 16 + 16, :]
        res_ref[256 + b * 16 : 272 + b * 16, :] = block.astype(F32)
    loop(n - 1, lambda d: ag_copy(d + 1).wait_send())
    loop(n - 1, lambda d: sb_copy(d + 1).wait_send())


def finish(res_ref, fo_ref, gstem_ref, gsp_ref, gtm_ref, bg_ref):
    bands = gstem_ref.shape[0]
    for t in range(2):
        part = res_ref[t * 128 : t * 128 + 128, :].reshape(4, 32, res_ref.shape[1])
        fo_ref[t] = jnp.swapaxes(part, 0, 1).astype(BF16)
        bg_ref[:, t, :] = res_ref[656 + t * 16 : 656 + t * 16 + bands, :]
    gstem_ref[...] = res_ref[640 : 640 + bands, :]
    for q in range(12):
        block = res_ref[256 + q * 32 : 288 + q * 32, :]
        if q < 9:
            gsp_ref[q] = block
        else:
            gtm_ref[q - 9] = block


def per_device(
    panels, panel_tile, panel_date, stem_weight, spatial_weight, temporal_weight, cotangent
):
    n = lax.axis_size("tile")
    nf = lax.axis_size("filt")
    n_slots, n_bands, cols = panels.shape
    n_dates, own, n_rows, _ = cotangent.shape
    chan = stem_weight.shape[1]
    bp = -(-24 // n)
    scale = 1.0 / math.sqrt(n_dates * n_rows * n * cols)
    ws = spatial_weight.transpose(0, 1, 3, 2).reshape(9, own, chan)
    wtm = temporal_weight.transpose(0, 2, 1)
    dma = pltpu.SemaphoreType.DMA
    vmem = pl.BlockSpec(memory_space=pltpu.VMEM)
    smem = pl.BlockSpec(memory_space=pltpu.SMEM)
    out = pl.pallas_call(
        functools.partial(kernel, n, nf, bp, scale),
        out_shape=jax.ShapeDtypeStruct((688, cols), F32),
        in_specs=[smem, smem, vmem, vmem, vmem, vmem, vmem],
        out_specs=vmem,
        scratch_shapes=[
            pltpu.VMEM((n_slots, 16, cols), F32),
            pltpu.VMEM((n, 32, cols), BF16),
            pltpu.VMEM((n, 32, cols), BF16),
            pltpu.VMEM((8, 32, cols), BF16),
            pltpu.VMEM((chan, 12 * chan), BF16),
            pltpu.VMEM((chan, 12 * chan), BF16),
            pltpu.VMEM((16, chan), BF16),
            pltpu.VMEM((cols, chan), F32),
            pltpu.VMEM((6, 2, chan, cols), BF16),
            pltpu.VMEM((3 * chan, 2 * 8 * cols), BF16),
            pltpu.VMEM((2 * chan, 4 * cols), BF16),
            pltpu.VMEM((chan, 2 * 6 * cols), BF16),
            pltpu.VMEM((3 * chan, 6 * cols), BF16),
            pltpu.VMEM((n, bp * 16, cols), BF16),
            pltpu.VMEM((n, bp * 16, cols), BF16),
            pltpu.VMEM((n, bp * 16, cols), BF16),
            pltpu.VMEM((16, cols), F32),
            pltpu.VMEM((nf, 16, cols), F32),
            pltpu.VMEM((16, cols), F32),
            pltpu.VMEM((n, 16, cols), F32),
            dma((n,)), dma((n,)), dma((8,)), dma((8,)), dma((nf,)), dma((nf,)),
            dma((nf,)), dma((nf,)), dma((nf,)), dma((nf,)), dma((nf,)), dma((nf,)),
            dma((n,)), dma((n,)), dma((n,)), dma((n,)), dma((nf,)), dma((nf,)), dma((n,)), dma((n,)),
        ],
        compiler_params=pltpu.CompilerParams(
            collective_id=0, has_side_effects=True, vmem_limit_bytes=40 * 1024 * 1024
        ),
    )(panel_tile.T, panel_date, panels.transpose(1, 0, 2), stem_weight, ws, wtm, cotangent.transpose(2, 0, 1, 3))
    features_out, grad_stem, gsp, gtm, bg = pl.pallas_call(
        finish,
        out_shape=(
            jax.ShapeDtypeStruct((n_dates, own, n_rows, cols), BF16),
            jax.ShapeDtypeStruct((n_bands, chan), F32),
            jax.ShapeDtypeStruct((9, own, chan), F32),
            jax.ShapeDtypeStruct((3, own, chan), F32),
            jax.ShapeDtypeStruct((n_bands, n_dates, cols), F32),
        ),
        in_specs=[vmem],
        out_specs=(vmem,) * 5,
    )(out)
    return (
        features_out,
        grad_stem,
        gsp.reshape(3, 3, own, chan).transpose(0, 1, 3, 2),
        gtm.transpose(0, 2, 1),
        bg.transpose(1, 0, 2),
    )


def solution(mesh):
    in_specs = (
        P("tile", None, "filt"),
        P("tile", None),
        P("tile"),
        P(),
        P(None, None, None, "filt"),
        P(None, None, "filt"),
        P(None, "filt", "tile", None),
    )
    out_specs = (
        P(None, "filt", "tile", None),
        P(),
        P(None, None, None, "filt"),
        P(None, None, "filt"),
        P(None, None, ("tile", "filt")),
    )
    return jax.shard_map(
        per_device, mesh=mesh, in_specs=in_specs, out_specs=out_specs, check_vma=False
    )
```

```python
import functools
import math

import jax
import jax.numpy as jnp
from jax import lax
from jax.experimental import pallas as pl
from jax.experimental.pallas import tpu as pltpu
from jax.sharding import PartitionSpec as P

MESH = pl.DeviceIdType.MESH
F32 = jnp.float32
BF16 = jnp.bfloat16


def loop(count, body):
    if count <= 8:
        for i in range(count):
            body(i)
    else:
        lax.fori_loop(0, count, lambda i, c: (body(i), c)[1], 0)


def total(count, term):
    if count <= 8:
        out = term(0)
        for i in range(1, count):
            out = out + term(i)
        return out
    return lax.fori_loop(1, count, lambda i, c: c + term(i), term(0))


def dot(a, b):
    return jnp.dot(a, b, preferred_element_type=F32)


def dot_t(a, b):
    return lax.dot_general(a, b, (((1,), (1,)), ((), ())), preferred_element_type=F32)


def shifted(block, offset):
    cols = block.shape[1]
    lane = lax.broadcasted_iota(jnp.int32, block.shape, 1)
    if offset == 1:
        return jnp.where(lane == cols - 1, 0.0, pltpu.roll(block, cols - 1, 1))
    return jnp.where(lane == 0, 0.0, pltpu.roll(block, 1, 1))


def kernel(
    n, nf, bp, scale,
    tile_ref, date_ref, panels_ref, stem_ref, ws_ref, wtm_ref, cot_ref,
    res_ref,
    pp, pan_out, pan_in, raw, wall, wback, stem16, stem_t, cot, feat, act, pre_g, pg3,
    rs_out, rs_in, ag, sa_out, sa, sb_out, sb,
    pan_s, pan_r, raw_s, raw_r, w_s, w_r, c_s, c_r, lo_s, lo_r, hi_s, hi_r,
    rs_s, rs_r, ag_s, ag_r, sa_s, sa_r, sb_s, sb_r,
):
    j = lax.axis_index("tile")
    f = lax.axis_index("filt")
    bands, n_slots = panels_ref.shape[0:2]
    own = ws_ref.shape[1]
    chan = own * nf
    cols = 128

    def tpeer(d):
        return lax.rem(j + d, n)

    def fpeer(d):
        return lax.rem(f + d, nf)

    def remote(src, dst, s, r, to):
        return pltpu.make_async_remote_copy(
            src_ref=src, dst_ref=dst, send_sem=s, recv_sem=r, device_id=to, device_id_type=MESH
        )

    barrier = pltpu.get_barrier_semaphore()

    def hello(t, g):
        pl.semaphore_signal(barrier, inc=1, device_id=(t, g), device_id_type=MESH)

    loop(n - 1, lambda d: hello(tpeer(d + 1), f))
    for d in range(1, nf):
        hello(j, fpeer(d))

    @pl.when(j > 0)
    def _():
        for d in range(1, nf):
            hello(j - 1, fpeer(d))

    @pl.when(j < n - 1)
    def _():
        for d in range(1, nf):
            hello(j + 1, fpeer(d))

    mine = pl.ds(pl.multiple_of(f * own, own), own)
    for q in range(12):
        wall[mine, q * chan : (q + 1) * chan] = ws_ref[q] if q < 9 else wtm_ref[q - 9]
    for t in range(2):
        for r in range(4):
            cot[1 + r, t, mine, :] = cot_ref[r, t]
    pad_rows = lax.broadcasted_iota(jnp.int32, (n_slots, 16, cols), 1)
    pp[...] = jnp.where(pad_rows == bands, 1.0, 0.0)
    for b in range(bands):
        pp[:, b, :] = panels_ref[b].astype(F32)

    def fill(k):
        def term(s):
            block = pp[s]
            here = tile_ref[0, s] == k
            first = jnp.where(here & (date_ref[s] == 0), 1.0, 0.0)
            second = jnp.where(here & (date_ref[s] == 1), 1.0, 0.0)
            return jnp.concatenate([block * first, block * second], axis=0)

        pan_out[k] = total(n_slots, term).astype(BF16)

    loop(n, fill)

    @pl.when(j == 0)
    def _():
        raw[0:2] = jnp.zeros((2, 32, cols), BF16)
        cot[0] = jnp.zeros((2, chan, cols), BF16)

    @pl.when(j == n - 1)
    def _():
        raw[6:8] = jnp.zeros((2, 32, cols), BF16)
        cot[5] = jnp.zeros((2, chan, cols), BF16)

    sides = jnp.where(j > 0, 1, 0) + jnp.where(j < n - 1, 1, 0)
    pl.semaphore_wait(barrier, n - 1 + (nf - 1) * (1 + sides))

    def pan_copy(d):
        k = tpeer(d)
        return remote(pan_out.at[k], pan_in.at[j], pan_s.at[d], pan_r.at[j], (k, f))

    def pan_wait(d):
        k = tpeer(d)
        remote(pan_out.at[k], pan_in.at[k], pan_s.at[d], pan_r.at[k], (k, f)).wait_recv()

    loop(n - 1, lambda d: pan_copy(d + 1).start())

    sib = f + 1 - 2 * lax.rem(f, 2)
    par = lax.rem(f + 2, nf)
    diag = lax.rem(sib + 2, nf)

    def group(g):
        return pl.ds(pl.multiple_of(g * own, own), own)

    def w_copy(to, slot):
        return remote(wall.at[mine], wall.at[mine], w_s.at[slot], w_r.at[f], (j, to))

    def c_copy(to, slot):
        return remote(cot.at[pl.ds(1, 4), :, mine, :], cot.at[pl.ds(1, 4), :, mine, :], c_s.at[slot], c_r.at[f], (j, to))

    def w_forward():
        at = wall.at[group(par)]
        return remote(at, at, w_s.at[2], w_r.at[par], (j, sib))

    def c_forward():
        at = cot.at[pl.ds(1, 4), :, group(par), :]
        return remote(at, at, c_s.at[2], c_r.at[par], (j, sib))

    def w_wait(g):
        remote(wall.at[mine], wall.at[group(g)], w_s.at[0], w_r.at[g], (j, par)).wait_recv()

    def c_wait(g):
        at = cot.at[pl.ds(1, 4), :, group(g), :]
        remote(cot.at[pl.ds(1, 4), :, mine, :], at, c_s.at[0], c_r.at[g], (j, par)).wait_recv()

    def lo_copy(d):
        return remote(cot.at[4, :, mine, :], cot.at[0, :, mine, :], lo_s.at[d], lo_r.at[f], (j + 1, fpeer(d)))

    def hi_copy(d):
        return remote(cot.at[1, :, mine, :], cot.at[5, :, mine, :], hi_s.at[d], hi_r.at[f], (j - 1, fpeer(d)))

    w_copy(par, 0).start()
    w_copy(sib, 1).start()
    c_copy(par, 0).start()
    c_copy(sib, 1).start()

    @pl.when(j < n - 1)
    def _():
        for d in range(nf):
            lo_copy(d).start()

    @pl.when(j > 0)
    def _():
        for d in range(nf):
            hi_copy(d).start()

    stem_t[...] = jnp.zeros((cols, chan), F32)
    stem_t[0:bands, :] = stem_ref[...].astype(F32)
    stem16[...] = stem_t[0:16, :].astype(BF16)
    stem_lhs = stem_t[...].T[:, 0:16].astype(BF16)

    pan_in[j] = pan_out[j]
    loop(n - 1, lambda d: pan_wait(d + 1))
    sums = total(n, lambda k: pan_in[k].astype(F32))
    row = jnp.concatenate(
        [
            sums[t * 16 : t * 16 + 16] / jnp.maximum(sums[t * 16 + bands : t * 16 + bands + 1], 1.0)
            for t in range(2)
        ],
        axis=0,
    ).astype(BF16)
    raw[2 + f] = row

    def raw_copy(d):
        return remote(raw.at[2 + f], raw.at[2 + f], raw_s.at[d], raw_r.at[2 + f], (j, fpeer(d)))

    def raw_down(d):
        return remote(raw.at[2 + f], raw.at[f - 2], raw_s.at[4 + d], raw_r.at[f - 2], (j + 1, fpeer(d)))

    def raw_up(d):
        return remote(raw.at[2 + f], raw.at[6 + f], raw_s.at[4 + d], raw_r.at[6 + f], (j - 1, fpeer(d)))

    for d in range(1, nf):
        raw_copy(d).start()
    goes_down = (f >= 2) & (j < n - 1)
    goes_up = (f < 2) & (j > 0)

    @pl.when(goes_down)
    def _():
        for d in range(nf):
            raw_down(d).start()

    @pl.when(goes_up)
    def _():
        for d in range(nf):
            raw_up(d).start()

    w_wait(par)
    w_forward().start()

    def raw_wait(slot):
        remote(raw.at[slot], raw.at[slot], raw_s.at[0], raw_r.at[slot], (j, fpeer(1))).wait_recv()

    for d in range(1, nf):
        raw_wait(2 + fpeer(d))

    @pl.when(j > 0)
    def _():
        raw_wait(0)
        raw_wait(1)

    @pl.when(j < n - 1)
    def _():
        raw_wait(6)
        raw_wait(7)

    for t in range(2):
        for r in range(8):
            block = dot(stem_lhs, raw[r, t * 16 : t * 16 + 16, :]).astype(BF16)
            at = (t * 8 + r) * cols
            wide = block.astype(F32)
            feat[0:chan, at : at + cols] = shifted(wide, -1).astype(BF16)
            feat[chan : 2 * chan, at : at + cols] = block
            feat[2 * chan : 3 * chan, at : at + cols] = shifted(wide, 1).astype(BF16)

    c_wait(par)
    c_forward().start()
    w_wait(sib)
    w_wait(diag)
    for q in range(12):
        block = wall[:, q * chan : (q + 1) * chan].astype(F32).T.astype(BF16)
        at = q if q < 9 else 9 + (11 - q)
        wback[:, at * chan : (at + 1) * chan] = block
    c_wait(sib)
    c_wait(diag)

    @pl.when(j > 0)
    def _():
        for g in range(nf):
            remote(cot.at[4, :, mine, :], cot.at[0, :, g * own : (g + 1) * own, :], lo_s.at[g], lo_r.at[g], (j - 1, g)).wait_recv()

    @pl.when(j < n - 1)
    def _():
        for g in range(nf):
            remote(cot.at[1, :, mine, :], cot.at[5, :, g * own : (g + 1) * own, :], hi_s.at[g], hi_r.at[g], (j + 1, g)).wait_recv()

    cot_rows = jnp.concatenate([cot[r].reshape(2 * chan, cols) for r in range(6)], axis=1)
    lane = lax.broadcasted_iota(jnp.int32, (chan, 6 * cols), 1)
    inside = ((lane >= cols) | (j > 0)) & ((lane < 5 * cols) | (j < n - 1))
    for t in range(2):
        pre = dot(wall[:, 0 : 3 * chan], feat[:, t * 1024 : t * 1024 + 768])
        for dy in (1, 2):
            at = t * 1024 + dy * cols
            pre = pre + dot(wall[:, dy * 3 * chan : (dy + 1) * 3 * chan], feat[:, at : at + 768])
        sigma = jax.nn.sigmoid(pre)
        act[t * chan : (t + 1) * chan, :] = (pre * sigma)[:, cols : 5 * cols].astype(BF16)
        act_grad = dot(wback[:, (10 - t) * chan : (12 - t) * chan], cot_rows)
        slope = sigma * (1.0 + pre * (1.0 - sigma))
        pre_g[:, t * 768 : (t + 1) * 768] = jnp.where(inside, act_grad * slope, 0.0).astype(BF16)

    def put(q, grad):
        for h in range(2):
            b = q * 2 + h
            rs_out[b // bp, (b % bp) * 16 : (b % bp) * 16 + 16, :] = grad[h * 16 : h * 16 + 16].astype(BF16)

    cot_own = [
        jnp.concatenate([cot[1 + r, t, mine, :] for r in range(4)], axis=1) for t in range(2)
    ]
    act0, act1 = act[0:chan, :], act[chan : 2 * chan, :]
    put(9, dot_t(cot_own[1], act0) * scale)
    put(10, (dot_t(cot_own[0], act0) + dot_t(cot_own[1], act1)) * scale)
    put(11, dot_t(cot_own[0], act1) * scale)
    pg_own = [pre_g[mine, t * 768 + cols : t * 768 + 5 * cols] for t in range(2)]
    for dy in range(3):
        at = (dy + 1) * cols
        grad = dot_t(pg_own[0], feat[:, at : at + 512])
        grad = grad + dot_t(pg_own[1], feat[:, 1024 + at : 1024 + at + 512])
        grad = grad * scale
        for dx in range(3):
            put(dy * 3 + dx, grad[:, dx * chan : (dx + 1) * chan])
    if n * bp > 24:
        used = -(-24 // bp)
        loop(n - used, lambda k: rs_out.__setitem__(used + k, jnp.zeros((bp * 16, cols), BF16)))

    def rs_copy(d):
        k = tpeer(d)
        return remote(rs_out.at[k], rs_in.at[j], rs_s.at[d], rs_r.at[j], (k, f))

    loop(n - 1, lambda d: rs_copy(d + 1).start())
    rs_in[j] = rs_out[j]

    for t in range(2):
        for r in range(3):
            at = pl.ds(pl.multiple_of(t * 768 + (f + r) * cols, cols), cols)
            block = pre_g[:, at]
            wide = block.astype(F32)
            to = (r * 2 + t) * cols
            pg3[0:chan, to : to + cols] = shifted(wide, 1).astype(BF16)
            pg3[chan : 2 * chan, to : to + cols] = block
            pg3[2 * chan : 3 * chan, to : to + cols] = shifted(wide, -1).astype(BF16)
    fgrad = jnp.concatenate([cot[1 + f, t].astype(F32) for t in range(2)], axis=1)
    for dy in range(3):
        at = (2 - dy) * 2 * cols
        fgrad = fgrad + dot(wback[:, dy * 3 * chan : (dy + 1) * 3 * chan], pg3[:, at : at + 2 * cols])
    upper = fgrad.astype(BF16)
    lower = (fgrad - upper.astype(F32)).astype(BF16)
    own_raw = raw[2 + f]
    raw_row = jnp.concatenate([own_raw[0:16], own_raw[16:32]], axis=1)
    sa_out[...] = (dot_t(raw_row, upper) + dot_t(raw_row, lower)) * scale

    def sa_copy(d):
        return remote(sa_out, sa.at[f], sa_s.at[d], sa_r.at[f], (j, fpeer(d)))

    for d in range(1, nf):
        sa_copy(d).start()
    sa[f] = sa_out[...]
    bgrad = dot(stem16[...], upper) + dot(stem16[...], lower)
    for t in range(2):
        res_ref[656 + t * 16 : 672 + t * 16, :] = bgrad[:, t * cols : (t + 1) * cols]

    wt_time = wall[mine, 9 * chan : 12 * chan]
    feat_own = pl.ds(pl.multiple_of(chan + f * own, own), own)
    for t in range(2):
        out = dot(wt_time[:, (1 - t) * chan : (3 - t) * chan], act[...])
        out = out + feat[feat_own, t * 1024 + 256 : t * 1024 + 768].astype(F32)
        for r in range(4):
            at = (t * 4 + r) * own
            res_ref[at : at + own, :] = out[:, r * cols : (r + 1) * cols]

    for d in range(1, nf):
        g = fpeer(d)
        remote(sa_out, sa.at[g], sa_s.at[d], sa_r.at[g], (j, g)).wait_recv()
    sb_out[...] = (sa[0] + sa[1]) + (sa[2] + sa[3])

    def sb_copy(d):
        k = tpeer(d)
        return remote(sb_out, sb.at[j], sb_s.at[d], sb_r.at[j], (k, f))

    loop(n - 1, lambda d: sb_copy(d + 1).start())
    sb[j] = sb_out[...]

    def rs_wait(d):
        k = tpeer(d)
        remote(rs_out.at[k], rs_in.at[k], rs_s.at[d], rs_r.at[k], (k, f)).wait_recv()

    loop(n - 1, lambda d: rs_wait(d + 1))
    ag[j] = total(n, lambda k: rs_in[k].astype(F32)).astype(BF16)

    def ag_copy(d):
        k = tpeer(d)
        return remote(ag.at[j], ag.at[j], ag_s.at[d], ag_r.at[j], (k, f))

    loop(n - 1, lambda d: ag_copy(d + 1).start())

    w_copy(par, 0).wait_send()
    w_copy(sib, 1).wait_send()
    w_forward().wait_send()
    c_copy(par, 0).wait_send()
    c_copy(sib, 1).wait_send()
    c_forward().wait_send()
    loop(n - 1, lambda d: pan_copy(d + 1).wait_send())
    for d in range(1, nf):
        raw_copy(d).wait_send()
        sa_copy(d).wait_send()

    @pl.when(j < n - 1)
    def _():
        for d in range(nf):
            lo_copy(d).wait_send()

    @pl.when(j > 0)
    def _():
        for d in range(nf):
            hi_copy(d).wait_send()

    @pl.when(goes_down)
    def _():
        for d in range(nf):
            raw_down(d).wait_send()

    @pl.when(goes_up)
    def _():
        for d in range(nf):
            raw_up(d).wait_send()

    loop(n - 1, lambda d: rs_copy(d + 1).wait_send())

    def sb_wait(d):
        k = tpeer(d)
        remote(sb_out, sb.at[k], sb_s.at[d], sb_r.at[k], (k, f)).wait_recv()

    loop(n - 1, lambda d: sb_wait(d + 1))
    res_ref[640:656, :] = total(n, lambda k: sb[k])

    def ag_wait(d):
        k = tpeer(d)
        remote(ag.at[k], ag.at[k], ag_s.at[d], ag_r.at[k], (k, f)).wait_recv()

    loop(n - 1, lambda d: ag_wait(d + 1))
    for b in range(24):
        block = ag[b // bp, (b % bp) * 16 : (b % bp) * 16 + 16, :]
        res_ref[256 + b * 16 : 272 + b * 16, :] = block.astype(F32)
    loop(n - 1, lambda d: ag_copy(d + 1).wait_send())
    loop(n - 1, lambda d: sb_copy(d + 1).wait_send())


def finish(res_ref, fo_ref, gstem_ref, gsp_ref, gtm_ref, bg_ref):
    bands = gstem_ref.shape[0]
    for t in range(2):
        part = res_ref[t * 128 : t * 128 + 128, :].reshape(4, 32, res_ref.shape[1])
        fo_ref[t] = jnp.swapaxes(part, 0, 1).astype(BF16)
        bg_ref[:, t, :] = res_ref[656 + t * 16 : 656 + t * 16 + bands, :]
    gstem_ref[...] = res_ref[640 : 640 + bands, :]
    for q in range(12):
        block = res_ref[256 + q * 32 : 288 + q * 32, :]
        if q < 9:
            gsp_ref[q] = block
        else:
            gtm_ref[q - 9] = block


def per_device(
    panels, panel_tile, panel_date, stem_weight, spatial_weight, temporal_weight, cotangent
):
    n = lax.axis_size("tile")
    nf = lax.axis_size("filt")
    n_slots, n_bands, cols = panels.shape
    n_dates, own, n_rows, _ = cotangent.shape
    chan = stem_weight.shape[1]
    bp = -(-24 // n)
    scale = 1.0 / math.sqrt(n_dates * n_rows * n * cols)
    ws = spatial_weight.transpose(0, 1, 3, 2).reshape(9, own, chan)
    wtm = temporal_weight.transpose(0, 2, 1)
    dma = pltpu.SemaphoreType.DMA
    vmem = pl.BlockSpec(memory_space=pltpu.VMEM)
    smem = pl.BlockSpec(memory_space=pltpu.SMEM)
    out = pl.pallas_call(
        functools.partial(kernel, n, nf, bp, scale),
        out_shape=jax.ShapeDtypeStruct((688, cols), F32),
        in_specs=[smem, smem, vmem, vmem, vmem, vmem, vmem],
        out_specs=vmem,
        scratch_shapes=[
            pltpu.VMEM((n_slots, 16, cols), F32),
            pltpu.VMEM((n, 32, cols), BF16),
            pltpu.VMEM((n, 32, cols), BF16),
            pltpu.VMEM((8, 32, cols), BF16),
            pltpu.VMEM((chan, 12 * chan), BF16),
            pltpu.VMEM((chan, 12 * chan), BF16),
            pltpu.VMEM((16, chan), BF16),
            pltpu.VMEM((cols, chan), F32),
            pltpu.VMEM((6, 2, chan, cols), BF16),
            pltpu.VMEM((3 * chan, 2 * 8 * cols), BF16),
            pltpu.VMEM((2 * chan, 4 * cols), BF16),
            pltpu.VMEM((chan, 2 * 6 * cols), BF16),
            pltpu.VMEM((3 * chan, 6 * cols), BF16),
            pltpu.VMEM((n, bp * 16, cols), BF16),
            pltpu.VMEM((n, bp * 16, cols), BF16),
            pltpu.VMEM((n, bp * 16, cols), BF16),
            pltpu.VMEM((16, cols), F32),
            pltpu.VMEM((nf, 16, cols), F32),
            pltpu.VMEM((16, cols), F32),
            pltpu.VMEM((n, 16, cols), F32),
            dma((n,)), dma((n,)), dma((8,)), dma((8,)), dma((nf,)), dma((nf,)),
            dma((nf,)), dma((nf,)), dma((nf,)), dma((nf,)), dma((nf,)), dma((nf,)),
            dma((n,)), dma((n,)), dma((n,)), dma((n,)), dma((nf,)), dma((nf,)), dma((n,)), dma((n,)),
        ],
        compiler_params=pltpu.CompilerParams(
            collective_id=0, has_side_effects=True, vmem_limit_bytes=16 * 1024 * 1024
        ),
    )(panel_tile.T, panel_date, panels.transpose(1, 0, 2), stem_weight, ws, wtm, cotangent.transpose(2, 0, 1, 3))
    features_out, grad_stem, gsp, gtm, bg = pl.pallas_call(
        finish,
        out_shape=(
            jax.ShapeDtypeStruct((n_dates, own, n_rows, cols), BF16),
            jax.ShapeDtypeStruct((n_bands, chan), F32),
            jax.ShapeDtypeStruct((9, own, chan), F32),
            jax.ShapeDtypeStruct((3, own, chan), F32),
            jax.ShapeDtypeStruct((n_bands, n_dates, cols), F32),
        ),
        in_specs=[vmem],
        out_specs=(vmem,) * 5,
        compiler_params=pltpu.CompilerParams(vmem_limit_bytes=8 * 1024 * 1024),
    )(out)
    return (
        features_out,
        grad_stem,
        gsp.reshape(3, 3, own, chan).transpose(0, 1, 3, 2),
        gtm.transpose(0, 2, 1),
        bg.transpose(1, 0, 2),
    )


def solution(mesh):
    in_specs = (
        P("tile", None, "filt"),
        P("tile", None),
        P("tile"),
        P(),
        P(None, None, None, "filt"),
        P(None, None, "filt"),
        P(None, "filt", "tile", None),
    )
    out_specs = (
        P(None, "filt", "tile", None),
        P(),
        P(None, None, None, "filt"),
        P(None, None, "filt"),
        P(None, None, ("tile", "filt")),
    )
    return jax.shard_map(
        per_device, mesh=mesh, in_specs=in_specs, out_specs=out_specs, check_vma=False
    )
```
